32 devices in a mesh: seq: 4 (over y, x), dp: 8 (over z, core).
Axes of the slice: x: 2, y: 2, z: 4, core: 2. Of those that a mesh axis runs over, the one named last changes fastest.
Arguments:
- sensors: bfloat16 [16384, 512], P(('seq', 'dp')), may hold values from -6 to 6
- slot_region: int32 [16384], P(('seq', 'dp')), may hold values from -1 to 255, as said below
- w_query: bfloat16 [512, 512], replicated, may hold values from -0.25 to 0.25
- w_key: bfloat16 [512, 128], replicated, may hold values from -0.25 to 0.25
- w_value: bfloat16 [512, 128], replicated, may hold values from -0.25 to 0.25
- w_out: bfloat16 [512, 512], replicated, may hold values from -0.25 to 0.25
- temper: float32 [8], replicated, may hold values from 16 to 48
- gain_attn: float32 [512], replicated, may hold values from 0.25 to 1.75
- w_inner: bfloat16 [512, 2048], replicated, may hold values from -0.25 to 0.25
- w_outer: bfloat16 [2048, 512], replicated, may hold values from -0.125 to 0.125
- gain_mlp: float32 [512], replicated, may hold values from 0.25 to 1.75
- gain_dec: float32 [512], replicated, may hold values from 0.25 to 1.75
- w_dec_in: bfloat16 [512, 512], replicated, may hold values from -0.25 to 0.25
- w_dec_out: bfloat16 [512, 512], replicated, may hold values from -0.25 to 0.25
Outputs:
- recon: bfloat16 [16384, 512], P(('seq', 'dp'))
The draws below stay inside these ranges and needn't reach their ends.
Inputs may be any that keep to these rules, and one draw needn't show every extreme that they name: `slot_region`: each tile of 16 slots holds 0 to 16 live sensors, live slots first; some tile of every device is full, and one owner receives full tiles from every device.
All inputs are finite; a program needn't handle non-finite values.
Results may differ from the reference program's by a relative error of at most 0.015.
Values may be sent and summed in bfloat16 or wider, within the bound.
No kernel may reach another device: no remote copies, remote signals or barrier semaphores. Data moves between devices by JAX's collectives and lax.ppermute only.
A program may use at most 128 MiB of HBM per device.

```python
import math
import jax
import jax.numpy as jnp
from jax import lax

D = 512
HEADS = 8
HEAD_DIM = 64
KV_HEADS = 2
FF = 2048
TILE = 16
REG_DEV = 256
SENSORS = 16384
N_SEQ = 4
N_DP = 8


def draw_slot_region(key, part):
    devices = N_SEQ * N_DP
    keys = jax.random.split(key, 6)
    owner_cap = jax.random.randint(keys[0], (devices,), TILE // 4, TILE + 1)
    live = jax.random.randint(keys[1], (devices, devices), 0, owner_cap[None, :] + 1)
    column = jnp.arange(devices, dtype=jnp.int32)[None, :]
    busy = jax.random.randint(keys[2], (), 0, devices)
    live = jnp.where(column == busy, TILE, live)
    picked = jax.random.randint(keys[3], (devices,), 0, devices)
    live = jnp.where(column == picked[:, None], TILE, live)
    position = jnp.arange(TILE, dtype=jnp.int32)[None, None, :]
    bound = jax.random.randint(keys[4], (devices, devices, TILE), 1, REG_DEV + 1)
    labels = jax.random.randint(keys[5], (devices, devices, TILE), 0, bound)
    return jnp.where(position < live[:, :, None], labels, -1).astype(jnp.int32).reshape(-1)


def shard_levels(own_key, shape, cuts, least, high):
    factor_of = 1.0
    for dim, shards_of in cuts:
        steps = jax.random.uniform(jax.random.fold_in(jax.random.fold_in(own_key, 6), dim), (shards_of,), jnp.float32, least / len(cuts), high / len(cuts))
        factor_of = factor_of * jnp.repeat(jnp.exp(steps), shape[dim] // shards_of).reshape((-1,) + (1,) * (len(shape) - 1 - dim))
    return factor_of


def centred(stream_key, dims, deviation, most, cuts=(), held_as=jnp.bfloat16):
    array = deviation * jax.random.normal(stream_key, dims, jnp.float32)
    if cuts:
        array = array * shard_levels(stream_key, dims, cuts, -0.22, 0.18)
    return jnp.clip(array, -most, most).astype(held_as)


def setup_inputs(seed: int = 0) -> dict:
    key_of = jax.random.split(jax.random.key(seed), 15)
    return {
        "sensors": centred(key_of[0], (SENSORS, D), 1.0, 6.0, ((0, 32),)),
        "slot_region": draw_slot_region(jax.random.fold_in(key_of[14], 71), 0),
        "w_query": centred(key_of[2], (D, HEADS * HEAD_DIM), D ** -0.5, 0.25),
        "w_key": centred(key_of[3], (D, KV_HEADS * HEAD_DIM), D ** -0.5, 0.25),
        "w_value": centred(key_of[4], (D, KV_HEADS * HEAD_DIM), D ** -0.5, 0.25),
        "w_out": centred(key_of[5], (HEADS * HEAD_DIM, D), (HEADS * HEAD_DIM) ** -0.5, 0.25),
        "temper": jnp.clip(jnp.exp(jax.random.uniform(key_of[6], (HEADS,), jnp.float32, math.log(16.0), math.log(48.0))), 16.0, 48.0),
        "gain_attn": jnp.clip(1.0 + 0.15 * jax.random.normal(key_of[7], (D,), jnp.float32), 0.25, 1.75),
        "w_inner": centred(key_of[8], (D, FF), D ** -0.5, 0.25),
        "w_outer": centred(key_of[9], (FF, D), FF ** -0.5, 0.125),
        "gain_mlp": jnp.clip(1.0 + 0.15 * jax.random.normal(key_of[10], (D,), jnp.float32), 0.25, 1.75),
        "gain_dec": jnp.clip(1.0 + 0.15 * jax.random.normal(key_of[11], (D,), jnp.float32), 0.25, 1.75),
        "w_dec_in": centred(key_of[12], (D, D), D ** -0.5, 0.25),
        "w_dec_out": centred(key_of[13], (D, D), D ** -0.5, 0.25),
    }


EPS = 1e-06

def rms_scale(values, gain):
    return values * lax.rsqrt(lax.optimization_barrier(jnp.mean(values * values, axis=-1, keepdims=True)) + EPS) * gain

def unit_heads(values, heads):
    shaped = values.reshape(values.shape[0], heads, -1)
    return shaped * lax.rsqrt(lax.optimization_barrier(jnp.mean(shaped * shaped, axis=-1, keepdims=True)) + EPS)

def to_half(values):
    return lax.optimization_barrier(values.astype(jnp.bfloat16))

def reference(sensors, slot_region, w_query, w_key, w_value, w_out, temper, gain_attn, w_inner, w_outer, gain_mlp, gain_dec, w_dec_in, w_dec_out):
    devices = N_SEQ * N_DP
    sen_dev = TILE * devices
    regions = REG_DEV * devices
    width = sensors.shape[1]
    feats = sensors.reshape(devices, sen_dev, width)
    labels = slot_region.reshape(devices, sen_dev)
    owner = (jnp.arange(sen_dev, dtype=jnp.int32) // TILE).astype(jnp.int32)

    def pool_step(carry, block):
        rows, local = block
        target = jnp.where(local >= 0, owner * REG_DEV + local, regions).astype(jnp.int32)
        sums = jax.ops.segment_sum(rows.astype(jnp.float32), target, num_segments=regions + 1)
        counts = jax.ops.segment_sum(jnp.ones(local.shape, jnp.float32), target, num_segments=regions + 1)
        return ((carry[0] + sums[:regions], carry[1] + counts[:regions]), None)
    start = (jnp.zeros((regions, width), jnp.float32), jnp.zeros((regions,), jnp.float32))
    (region_sum, count), _ = lax.scan(pool_step, start, (feats, labels))
    pooled = region_sum / (1.0 + count)[:, None]
    attn_in = to_half(rms_scale(pooled, gain_attn))
    query_unit = to_half(unit_heads(jnp.dot(attn_in, w_query, preferred_element_type=jnp.float32), HEADS))
    key_unit = to_half(unit_heads(jnp.dot(attn_in, w_key, preferred_element_type=jnp.float32), KV_HEADS))
    value = to_half(jnp.dot(attn_in, w_value, preferred_element_type=jnp.float32)).reshape(regions, KV_HEADS, HEAD_DIM)
    group = HEADS // KV_HEADS
    qblock = math.gcd(regions, 256)
    grouped = query_unit.reshape(regions // qblock, qblock, KV_HEADS, group, HEAD_DIM)
    scale = (temper / HEAD_DIM).reshape(KV_HEADS, group, 1, 1)
    key_wide = key_unit.astype(jnp.float32)
    value_wide = value.astype(jnp.float32)

    def attend(block):
        scores = jnp.einsum('rgjd,kgd->gjrk', block.astype(jnp.float32), key_wide)
        weight = jnp.exp(scores * scale)
        total = lax.optimization_barrier(jnp.sum(weight, axis=-1))
        summed = jnp.einsum('gjrk,kgd->gjrd', to_half(weight).astype(jnp.float32), value_wide)
        result = summed / total[..., None]
        return jnp.transpose(result, (2, 0, 1, 3)).reshape(block.shape[0], HEADS * HEAD_DIM)
    attended = to_half(lax.map(attend, grouped).reshape(regions, HEADS * HEAD_DIM))
    hidden_one = pooled + jnp.dot(attended, w_out, preferred_element_type=jnp.float32)
    mlp_in = to_half(rms_scale(hidden_one, gain_mlp))
    inner = to_half(jax.nn.gelu(jnp.dot(mlp_in, w_inner, preferred_element_type=jnp.float32)))
    region_out = (hidden_one + jnp.dot(inner, w_outer, preferred_element_type=jnp.float32)).astype(jnp.bfloat16)

    def decode(block):
        rows, local = block
        target = jnp.clip(owner * REG_DEV + local, 0, regions - 1).astype(jnp.int32)
        back = jnp.take(region_out, target, axis=0)
        dec_in = to_half(rms_scale(back.astype(jnp.float32) + rows.astype(jnp.float32), gain_dec))
        dec_hidden = to_half(jax.nn.gelu(jnp.dot(dec_in, w_dec_in, preferred_element_type=jnp.float32)))
        result = jnp.dot(dec_hidden, w_dec_out, preferred_element_type=jnp.float32)
        return jnp.where((local >= 0)[:, None], result, 0.0).astype(jnp.bfloat16)
    return lax.map(decode, (feats, labels)).reshape(devices * sen_dev, width)
```

```python
import functools
import math

import jax
import jax.numpy as jnp
from jax import lax
from jax.experimental import pallas as pl
from jax.experimental.pallas import tpu as pltpu
from jax.sharding import PartitionSpec as P

HEADS = 8
HEAD_DIM = 64
KV_HEADS = 2
GROUP = HEADS // KV_HEADS
REG_DEV = 256
LANES = 128
EPS = 1e-06
AXES = ("seq", "dp")
F32 = jnp.float32
BF16 = jnp.bfloat16
NT = (((1,), (1,)), ((), ()))
TN = (((0,), (0,)), ((), ()))

VMEM = pl.BlockSpec(memory_space=pltpu.VMEM)
SMEM = pl.BlockSpec(memory_space=pltpu.SMEM)
PARAMS = pltpu.CompilerParams(vmem_limit_bytes=40 * 1024 * 1024)


def mm(a, b):
    return jnp.dot(a, b, preferred_element_type=F32)


def rms(values):
    return values * lax.rsqrt(jnp.mean(values * values, axis=-1, keepdims=True) + EPS)


def pack_kernel(tile, me_ref, sensors_ref, labels_ref, out_ref):
    per_row = LANES // tile
    blocks = sensors_ref.shape[1] // LANES
    tiles = out_ref.shape[0]
    mine = lax.rem(me_ref[0], per_row)
    labels = (labels_ref[...] + 1).astype(F32)
    lane = lax.broadcasted_iota(jnp.int32, labels.shape, 1)
    own_lanes = (lane // tile) == mine
    for k in range(per_row):
        shift = lax.rem(mine - k + per_row, per_row) * tile
        rolled = jnp.where(own_lanes, pltpu.roll(labels, shift, 1), 0.0)
        for g in range(tiles // per_row):
            t = g * per_row + k
            row = jnp.broadcast_to(rolled[g : g + 1, :], (8, LANES)).astype(BF16)
            rows = sensors_ref[t * tile : (t + 1) * tile, :]
            parts = [rows[:, c * LANES : (c + 1) * LANES] for c in range(blocks)]
            out_ref[t] = jnp.concatenate(parts + [row], axis=0)


def pool_kernel(
    tile, core_ref, got_ref, w_q_ref, w_kv_ref, q_scale_ref, gain_ref, pooled_ref, member_ref, keep_ref, send_ref
):
    tiles, _, _ = got_ref.shape
    per_row = LANES // tile
    width = pooled_ref.shape[1]
    blocks = width // LANES
    slots = tiles * tile
    regions = lax.broadcasted_iota(jnp.int32, (REG_DEV, LANES), 0).astype(F32) + 1.0
    count = jnp.zeros((REG_DEV, 1), F32)
    for g in range(tiles // per_row):
        row = got_ref[g * per_row, tile * blocks : tile * blocks + 8, :].astype(F32)
        for k in range(1, per_row):
            row = row + got_ref[g * per_row + k, tile * blocks : tile * blocks + 8, :].astype(F32)
        hit = jnp.where(regions == row[0:1, :], 1.0, 0.0)
        count = count + jnp.sum(hit, axis=1, keepdims=True)
        member_ref[:, g * LANES : (g + 1) * LANES] = hit.astype(BF16)
    members = member_ref[...]
    sums = [
        mm(members, got_ref[:, c * tile : (c + 1) * tile, :].reshape(slots, LANES))
        for c in range(blocks)
    ]
    pooled = jnp.concatenate(sums, axis=1) * (1.0 / (1.0 + count))
    pooled_ref[...] = pooled
    attn_in = (rms(pooled) * gain_ref[...]).astype(BF16)
    at = lax.broadcasted_iota(jnp.int32, (LANES, LANES), 0) // HEAD_DIM
    to = lax.broadcasted_iota(jnp.int32, (LANES, LANES), 1) // HEAD_DIM
    mean_heads = jnp.where(at == to, 1.0 / HEAD_DIM, 0.0).astype(BF16)
    low = lax.broadcasted_iota(jnp.int32, (REG_DEV, LANES), 1) < HEAD_DIM
    core = core_ref[0]

    def put(g, part, value):
        cols = slice(part * LANES, (part + 1) * LANES)

        @pl.when(core == g)
        def _():
            keep_ref[:, cols] = value

        @pl.when(core != g)
        def _():
            send_ref[:, cols] = value

    query = mm(attn_in, w_q_ref[...])
    for h in range(HEADS):
        values = query[:, h * LANES : (h + 1) * LANES]
        square = mm((values * values).astype(BF16), mean_heads)
        unit = values * lax.rsqrt(square + EPS) * q_scale_ref[:, h * LANES : (h + 1) * LANES]
        put(h // GROUP, h % GROUP, unit.astype(BF16))
    keyval = mm(attn_in, w_kv_ref[...])
    for g in range(KV_HEADS):
        values = keyval[:, g * LANES : (g + 1) * LANES]
        square = mm((values * values).astype(BF16), mean_heads)
        unit = values * jnp.where(low, lax.rsqrt(square + EPS), 1.0)
        put(g, GROUP, unit.astype(BF16))


def attend_kernel(n_kv, first, last, key_block, *refs):
    slabs, kvs = refs[:2], refs[2 : 2 + n_kv]
    rest = refs[2 + n_kv :]
    if first:
        (acc_ref,) = rest
    elif last:
        acc_in, keep_ref, send_ref, acc_ref = rest
    else:
        acc_in, acc_ref = rest
    if first:
        acc_ref[...] = jnp.zeros_like(acc_ref)
    else:
        acc_ref[...] = acc_in[...]
    for kv_ref in kvs:
        block = math.gcd(kv_ref.shape[0], key_block)

        def step(i, _, kv_ref=kv_ref, block=block):
            kv = kv_ref[pl.ds(pl.multiple_of(i * block, block), block), :]
            low = lax.broadcasted_iota(jnp.int32, kv.shape, 1) < HEAD_DIM
            ones_value = jnp.where(low, jnp.ones_like(kv), kv)
            for r in range(2):
                for h in range(GROUP):
                    q = slabs[r][:, h * LANES : (h + 1) * LANES]
                    score = lax.dot_general(q, kv, NT, preferred_element_type=F32)
                    weight = jnp.exp2(score).astype(BF16)
                    acc_ref[r, h] += mm(weight, ones_value)
            return 0

        lax.fori_loop(0, kv_ref.shape[0] // block, step, 0)
    if last:
        low = lax.broadcasted_iota(jnp.int32, (REG_DEV, LANES), 1) < HEAD_DIM
        for r, out_ref in enumerate((keep_ref, send_ref)):
            for j in range(GROUP // 2):
                a, b = acc_ref[r, 2 * j], acc_ref[r, 2 * j + 1]
                num = jnp.where(low, pltpu.roll(a, HEAD_DIM, 1), b)
                den = jnp.where(low, a, pltpu.roll(b, HEAD_DIM, 1))
                out_ref[:, j * LANES : (j + 1) * LANES] = (num / den).astype(BF16)


def post_kernel(
    core_ref, mine_ref, other_ref, pooled_ref, member_ref, w_out_ref, gain_ref, w_inner_ref, w_outer_ref, out_ref
):
    half = mine_ref.shape[1]
    core = core_ref[0]
    own = pl.ds(pl.multiple_of(core * half, half), half)
    far = pl.ds(pl.multiple_of((1 - core) * half, half), half)
    hidden = (
        pooled_ref[...] + mm(mine_ref[...], w_out_ref[own, :]) + mm(other_ref[...], w_out_ref[far, :])
    )
    mlp_in = (rms(hidden) * gain_ref[...]).astype(BF16)
    inner = jax.nn.gelu(mm(mlp_in, w_inner_ref[...])).astype(BF16)
    region_out = (hidden + mm(inner, w_outer_ref[...])).astype(BF16)
    slots = member_ref.shape[1]
    block = math.gcd(slots, 512)
    for i in range(slots // block):
        rows = slice(i * block, (i + 1) * block)
        out_ref[rows, :] = lax.dot_general(
            member_ref[:, rows], region_out, TN, preferred_element_type=F32
        ).astype(BF16)


def decode_kernel(back_ref, sensors_ref, live_ref, gain_ref, w_in_ref, w_out_ref, out_ref):
    total = back_ref[...].astype(F32) + sensors_ref[...].astype(F32)
    dec_in = (rms(total) * gain_ref[...]).astype(BF16)
    hidden = jax.nn.gelu(mm(dec_in, w_in_ref[...])).astype(BF16)
    result = mm(hidden, w_out_ref[...])
    out_ref[...] = jnp.where(live_ref[...] > 0.0, result, 0.0).astype(BF16)


def local(
    sensors,
    slot_region,
    w_query,
    w_key,
    w_value,
    w_out,
    temper,
    gain_attn,
    w_inner,
    w_outer,
    gain_mlp,
    gain_dec,
    w_dec_in,
    w_dec_out,
):
    devices = lax.axis_size(AXES)
    sen_dev, width = sensors.shape
    tile = sen_dev // devices
    me = lax.axis_index(AXES).astype(jnp.int32).reshape(1)
    core = lax.rem(me, 2)
    bits = devices.bit_length() - 1
    pay_rows = tile * (width // LANES) + 8

    def flipped(value, mask):
        return lax.ppermute(value, AXES, [(i, i ^ mask) for i in range(devices)])

    payload = pl.pallas_call(
        functools.partial(pack_kernel, tile),
        out_shape=jax.ShapeDtypeStruct((devices, pay_rows, LANES), BF16),
        in_specs=[SMEM, VMEM, VMEM],
        out_specs=VMEM,
        compiler_params=PARAMS,
        name="pack",
    )(me, sensors, slot_region.reshape(-1, LANES))
    got = lax.all_to_all(payload, AXES, split_axis=0, concat_axis=0, tiled=True)

    w_q = jnp.pad(w_query.reshape(width, HEADS, HEAD_DIM), ((0, 0), (0, 0), (0, LANES - HEAD_DIM)))
    w_q = w_q.reshape(width, HEADS * LANES)
    w_kv = jnp.stack(
        [w_key.reshape(width, KV_HEADS, HEAD_DIM), w_value.reshape(width, KV_HEADS, HEAD_DIM)], axis=2
    ).reshape(width, KV_HEADS * LANES)
    q_scale = jnp.repeat(temper * (math.log2(math.e) / HEAD_DIM), LANES).reshape(1, HEADS * LANES)
    live = (slot_region >= 0).astype(F32).reshape(sen_dev, 1)

    slab = (GROUP + 1) * LANES
    pooled, members, keep, send = pl.pallas_call(
        functools.partial(pool_kernel, tile),
        out_shape=(
            jax.ShapeDtypeStruct((REG_DEV, width), F32),
            jax.ShapeDtypeStruct((REG_DEV, sen_dev), BF16),
            jax.ShapeDtypeStruct((REG_DEV, slab), BF16),
            jax.ShapeDtypeStruct((REG_DEV, slab), BF16),
        ),
        in_specs=[SMEM] + [VMEM] * 5,
        out_specs=(VMEM,) * 4,
        compiler_params=PARAMS,
        name="pool",
    )(core, got, w_q, w_kv, q_scale, gain_attn.reshape(1, width))
    other = flipped(send, 1)

    def attend(kvs, acc=None, last=False):
        keys = sum(kv.shape[0] for kv in kvs)
        acc_shape = (2, GROUP, REG_DEV, LANES)
        half = jax.ShapeDtypeStruct((REG_DEV, GROUP * HEAD_DIM), BF16)
        work = 2 * GROUP * REG_DEV * keys
        return pl.pallas_call(
            functools.partial(attend_kernel, len(kvs), acc is None, last, 512),
            out_shape=(half, half) if last else jax.ShapeDtypeStruct(acc_shape, F32),
            in_specs=[VMEM] * (2 + len(kvs) + (acc is not None)),
            out_specs=(VMEM, VMEM) if last else VMEM,
            scratch_shapes=[pltpu.VMEM(acc_shape, F32)] if last else [],
            compiler_params=PARAMS,
            cost_estimate=pl.CostEstimate(
                flops=work * 4 * 256, bytes_accessed=keys * 2 * LANES, transcendentals=work
            ),
            name="attend",
        )(keep, other, *kvs, *(() if acc is None else (acc,)))

    held = jnp.concatenate([keep[:, GROUP * LANES :], other[:, GROUP * LANES :]], axis=0)
    acc = None
    for bit in range(bits - 3, 0, -1):
        came = flipped(held, 1 << bit)
        acc = attend([held] if acc is None else [newest], acc)
        newest = came
        held = jnp.concatenate([held, came], axis=0)
    one, two = 1 << (bits - 2), 1 << (bits - 1)
    came_one, came_two = flipped(held, one), flipped(held, two)
    acc = attend([newest], acc)
    half = held.shape[0] // 2
    far_one, far_two = flipped(came_two[:half], one), flipped(came_one[half:], two)
    acc = attend([came_one, came_two], acc)
    mine, theirs = attend([far_one, far_two], acc, last=True)
    other_heads = flipped(theirs, 1)

    back = pl.pallas_call(
        post_kernel,
        out_shape=jax.ShapeDtypeStruct((sen_dev, width), BF16),
        in_specs=[SMEM] + [VMEM] * 8,
        out_specs=VMEM,
        compiler_params=PARAMS,
        name="post",
    )(core, mine, other_heads, pooled, members, w_out, gain_mlp.reshape(1, width), w_inner, w_outer)
    returned = lax.all_to_all(
        back.reshape(devices, tile, width), AXES, split_axis=0, concat_axis=0, tiled=True
    ).reshape(sen_dev, width)

    rows = math.gcd(sen_dev, 512)
    by_rows = pl.BlockSpec((rows, width), lambda i: (i, 0))
    whole = lambda shape: pl.BlockSpec(shape, lambda i: (0, 0))
    return pl.pallas_call(
        decode_kernel,
        grid=(sen_dev // rows,),
        out_shape=jax.ShapeDtypeStruct((sen_dev, width), BF16),
        in_specs=[
            by_rows,
            by_rows,
            pl.BlockSpec((rows, 1), lambda i: (i, 0)),
            whole((1, width)),
            whole(w_dec_in.shape),
            whole(w_dec_out.shape),
        ],
        out_specs=by_rows,
        compiler_params=PARAMS,
        name="decode",
    )(returned, sensors, live, gain_dec.reshape(1, width), w_dec_in, w_dec_out)


def solution(mesh):
    placed = (P(AXES, None), P(AXES)) + (P(),) * 12
    return jax.shard_map(
        local, mesh=mesh, in_specs=placed, out_specs=P(AXES, None), check_vma=False
    )
```

```python
import functools
import math

import jax
import jax.numpy as jnp
from jax import lax
from jax.experimental import pallas as pl
from jax.experimental.pallas import tpu as pltpu
from jax.sharding import PartitionSpec as P

HEADS = 8
HEAD_DIM = 64
KV_HEADS = 2
GROUP = HEADS // KV_HEADS
REG_DEV = 256
LANES = 128
EPS = 1e-06
AXES = ("seq", "dp")
F32 = jnp.float32
BF16 = jnp.bfloat16
NT = (((1,), (1,)), ((), ()))
TN = (((0,), (0,)), ((), ()))

VMEM = pl.BlockSpec(memory_space=pltpu.VMEM)
SMEM = pl.BlockSpec(memory_space=pltpu.SMEM)
PARAMS = pltpu.CompilerParams(vmem_limit_bytes=40 * 1024 * 1024)


def mm(a, b):
    return jnp.dot(a, b, preferred_element_type=F32)


def rms(values):
    return values * lax.rsqrt(jnp.mean(values * values, axis=-1, keepdims=True) + EPS)


def pack_kernel(tile, me_ref, sensors_ref, labels_ref, out_ref):
    per_row = LANES // tile
    blocks = sensors_ref.shape[1] // LANES
    tiles = out_ref.shape[0]
    mine = lax.rem(me_ref[0], per_row)
    labels = (labels_ref[...] + 1).astype(F32)
    lane = lax.broadcasted_iota(jnp.int32, labels.shape, 1)
    own_lanes = (lane // tile) == mine
    for k in range(per_row):
        shift = lax.rem(mine - k + per_row, per_row) * tile
        rolled = jnp.where(own_lanes, pltpu.roll(labels, shift, 1), 0.0)
        for g in range(tiles // per_row):
            t = g * per_row + k
            row = jnp.broadcast_to(rolled[g : g + 1, :], (8, LANES)).astype(BF16)
            rows = sensors_ref[t * tile : (t + 1) * tile, :]
            parts = [rows[:, c * LANES : (c + 1) * LANES] for c in range(blocks)]
            out_ref[t] = jnp.concatenate(parts + [row], axis=0)


def pool_kernel(
    tile, core_ref, got_ref, w_q_ref, w_kv_ref, q_scale_ref, gain_ref, pooled_ref, member_ref, keep_ref, send_ref
):
    tiles, _, _ = got_ref.shape
    per_row = LANES // tile
    width = pooled_ref.shape[1]
    blocks = width // LANES
    slots = tiles * tile
    regions = lax.broadcasted_iota(jnp.int32, (REG_DEV, LANES), 0).astype(F32) + 1.0
    count = jnp.zeros((REG_DEV, 1), F32)
    for g in range(tiles // per_row):
        row = got_ref[g * per_row, tile * blocks : tile * blocks + 8, :].astype(F32)
        for k in range(1, per_row):
            row = row + got_ref[g * per_row + k, tile * blocks : tile * blocks + 8, :].astype(F32)
        hit = jnp.where(regions == row[0:1, :], 1.0, 0.0)
        count = count + jnp.sum(hit, axis=1, keepdims=True)
        member_ref[:, g * LANES : (g + 1) * LANES] = hit.astype(BF16)
    members = member_ref[...]
    sums = [
        mm(members, got_ref[:, c * tile : (c + 1) * tile, :].reshape(slots, LANES))
        for c in range(blocks)
    ]
    pooled = jnp.concatenate(sums, axis=1) * (1.0 / (1.0 + count))
    pooled_ref[...] = pooled
    attn_in = (rms(pooled) * gain_ref[...]).astype(BF16)
    at = lax.broadcasted_iota(jnp.int32, (LANES, LANES), 0) // HEAD_DIM
    to = lax.broadcasted_iota(jnp.int32, (LANES, LANES), 1) // HEAD_DIM
    mean_heads = jnp.where(at == to, 1.0 / HEAD_DIM, 0.0).astype(BF16)
    low = lax.broadcasted_iota(jnp.int32, (REG_DEV, LANES), 1) < HEAD_DIM
    core = core_ref[0]

    def put(g, part, value):
        cols = slice(part * LANES, (part + 1) * LANES)

        @pl.when(core == g)
        def _():
            keep_ref[:, cols] = value

        @pl.when(core != g)
        def _():
            send_ref[:, cols] = value

    query = mm(attn_in, w_q_ref[...])
    for h in range(HEADS):
        values = query[:, h * LANES : (h + 1) * LANES]
        square = mm((values * values).astype(BF16), mean_heads)
        unit = values * lax.rsqrt(square + EPS) * q_scale_ref[:, h * LANES : (h + 1) * LANES]
        put(h // GROUP, h % GROUP, unit.astype(BF16))
    keyval = mm(attn_in, w_kv_ref[...])
    for g in range(KV_HEADS):
        values = keyval[:, g * LANES : (g + 1) * LANES]
        square = mm((values * values).astype(BF16), mean_heads)
        unit = values * jnp.where(low, lax.rsqrt(square + EPS), 1.0)
        put(g, GROUP, unit.astype(BF16))


def attend_kernel(parts, first, last, *refs):
    slabs, kvs = refs[:2], refs[2 : 2 + parts]
    rest = refs[2 + parts :]
    key_ref, value_ref = rest[-2:]
    acc_in = None if first else rest[0]
    acc_ref = rest[-3]
    at = 0
    for kv_ref in kvs:
        kv = kv_ref[...]
        rows = kv.shape[0]
        low = lax.broadcasted_iota(jnp.int32, kv.shape, 1) < HEAD_DIM
        key_ref[at : at + rows, :] = kv
        value_ref[at : at + rows, :] = jnp.where(low, jnp.ones_like(kv), kv)
        at += rows
    block = max(n for n in range(REG_DEV, 2561, REG_DEV) if at % n == 0)

    def step(i, old_ref):
        keys = pl.ds(pl.multiple_of(i * block, block), block)
        for r in range(2):
            for h in range(GROUP):
                q = slabs[r][:, h * LANES : (h + 1) * LANES]
                score = lax.dot_general(q, key_ref[keys, :], NT, preferred_element_type=F32)
                new = mm(jnp.exp2(score).astype(BF16), value_ref[keys, :])
                acc_ref[r, h] = new if old_ref is None else old_ref[r, h] + new

    step(0, acc_in)
    if at > block:

        def body(i, carry):
            step(i, acc_ref)
            return carry

        lax.fori_loop(1, at // block, body, 0)
    if last:
        low = lax.broadcasted_iota(jnp.int32, (REG_DEV, LANES), 1) < HEAD_DIM
        for r, out_ref in enumerate(rest[1:3]):
            for j in range(GROUP // 2):
                a, b = acc_ref[r, 2 * j], acc_ref[r, 2 * j + 1]
                num = jnp.where(low, pltpu.roll(a, HEAD_DIM, 1), b)
                den = jnp.where(low, a, pltpu.roll(b, HEAD_DIM, 1))
                out_ref[:, j * LANES : (j + 1) * LANES] = (num / den).astype(BF16)


def post_kernel(
    core_ref, mine_ref, other_ref, pooled_ref, member_ref, w_out_ref, gain_ref, w_inner_ref, w_outer_ref, out_ref
):
    half = mine_ref.shape[1]
    core = core_ref[0]
    own = pl.ds(pl.multiple_of(core * half, half), half)
    far = pl.ds(pl.multiple_of((1 - core) * half, half), half)
    hidden = (
        pooled_ref[...] + mm(mine_ref[...], w_out_ref[own, :]) + mm(other_ref[...], w_out_ref[far, :])
    )
    mlp_in = (rms(hidden) * gain_ref[...]).astype(BF16)
    inner = jax.nn.gelu(mm(mlp_in, w_inner_ref[...])).astype(BF16)
    region_out = (hidden + mm(inner, w_outer_ref[...])).astype(BF16)
    slots = member_ref.shape[1]
    block = math.gcd(slots, 512)
    for i in range(slots // block):
        rows = slice(i * block, (i + 1) * block)
        out_ref[rows, :] = lax.dot_general(
            member_ref[:, rows], region_out, TN, preferred_element_type=F32
        ).astype(BF16)


def decode_kernel(back_ref, sensors_ref, live_ref, gain_ref, w_in_ref, w_out_ref, out_ref):
    total = back_ref[...].astype(F32) + sensors_ref[...].astype(F32)
    dec_in = (rms(total) * gain_ref[...]).astype(BF16)
    hidden = jax.nn.gelu(mm(dec_in, w_in_ref[...])).astype(BF16)
    result = mm(hidden, w_out_ref[...])
    out_ref[...] = jnp.where(live_ref[...] > 0.0, result, 0.0).astype(BF16)


def local(
    sensors,
    slot_region,
    w_query,
    w_key,
    w_value,
    w_out,
    temper,
    gain_attn,
    w_inner,
    w_outer,
    gain_mlp,
    gain_dec,
    w_dec_in,
    w_dec_out,
):
    devices = lax.axis_size(AXES)
    sen_dev, width = sensors.shape
    tile = sen_dev // devices
    me = lax.axis_index(AXES).astype(jnp.int32).reshape(1)
    core = lax.rem(me, 2)
    bits = devices.bit_length() - 1
    pay_rows = tile * (width // LANES) + 8

    def flipped(value, mask):
        return lax.ppermute(value, AXES, [(i, i ^ mask) for i in range(devices)])

    payload = pl.pallas_call(
        functools.partial(pack_kernel, tile),
        out_shape=jax.ShapeDtypeStruct((devices, pay_rows, LANES), BF16),
        in_specs=[SMEM, VMEM, VMEM],
        out_specs=VMEM,
        compiler_params=PARAMS,
        name="pack",
    )(me, sensors, slot_region.reshape(-1, LANES))
    got = lax.all_to_all(payload, AXES, split_axis=0, concat_axis=0, tiled=True)

    w_q = jnp.pad(w_query.reshape(width, HEADS, HEAD_DIM), ((0, 0), (0, 0), (0, LANES - HEAD_DIM)))
    w_q = w_q.reshape(width, HEADS * LANES)
    w_kv = jnp.stack(
        [w_key.reshape(width, KV_HEADS, HEAD_DIM), w_value.reshape(width, KV_HEADS, HEAD_DIM)], axis=2
    ).reshape(width, KV_HEADS * LANES)
    q_scale = jnp.repeat(temper * (math.log2(math.e) / HEAD_DIM), LANES).reshape(1, HEADS * LANES)
    live = (slot_region >= 0).astype(F32).reshape(sen_dev, 1)

    slab = (GROUP + 1) * LANES
    pooled, members, keep, send = pl.pallas_call(
        functools.partial(pool_kernel, tile),
        out_shape=(
            jax.ShapeDtypeStruct((REG_DEV, width), F32),
            jax.ShapeDtypeStruct((REG_DEV, sen_dev), BF16),
            jax.ShapeDtypeStruct((REG_DEV, slab), BF16),
            jax.ShapeDtypeStruct((REG_DEV, slab), BF16),
        ),
        in_specs=[SMEM] + [VMEM] * 5,
        out_specs=(VMEM,) * 4,
        compiler_params=PARAMS,
        name="pool",
    )(core, got, w_q, w_kv, q_scale, gain_attn.reshape(1, width))
    other = flipped(send, 1)

    def attend(parts, acc, last):
        keys = sum(part.shape[0] for part in parts)
        acc_shape = (2, GROUP, REG_DEV, LANES)
        half = jax.ShapeDtypeStruct((REG_DEV, GROUP * HEAD_DIM), BF16)
        work = 2 * GROUP * REG_DEV * keys
        return pl.pallas_call(
            functools.partial(attend_kernel, len(parts), acc is None, last),
            out_shape=(half, half) if last else jax.ShapeDtypeStruct(acc_shape, F32),
            in_specs=[VMEM] * (2 + len(parts) + (acc is not None)),
            out_specs=(VMEM, VMEM) if last else VMEM,
            scratch_shapes=([pltpu.VMEM(acc_shape, F32)] if last else [])
            + [pltpu.VMEM((keys, LANES), BF16)] * 2,
            compiler_params=PARAMS,
            cost_estimate=pl.CostEstimate(
                flops=work * 4 * 256, bytes_accessed=keys * 2 * LANES, transcendentals=work
            ),
            name="attend",
        )(keep, other, *parts, *(() if acc is None else (acc,)))

    one, two = 1 << (bits - 2), 1 << (bits - 1)
    own = jnp.concatenate([keep[:, GROUP * LANES :], other[:, GROUP * LANES :]], axis=0)
    line, fresh, sides, ready, acc = [own], [own], [], [own], None
    steps = list(range(bits - 3, 0, -1))
    while fresh or sides:
        along = [flipped(part, 1 << steps[0]) for part in line] if steps else []
        steps = steps[1:]
        first = [flipped(part, one) for part in fresh]
        corner = [flipped(b, one) for i, (a, b) in enumerate(sides) if i % 2 == 0]
        second = [flipped(part, two) for part in fresh]
        corner += [flipped(a, two) for i, (a, b) in enumerate(sides) if i % 2 == 1]
        acc = attend(ready, acc, False)
        acc, along, first, second = lax.optimization_barrier((acc, along, first, second))
        ready = along + first + second + corner
        line, fresh, sides = line + along, along, list(zip(first, second))
    mine, theirs = attend(ready, acc, True)
    other_heads = flipped(theirs, 1)

    back = pl.pallas_call(
        post_kernel,
        out_shape=jax.ShapeDtypeStruct((sen_dev, width), BF16),
        in_specs=[SMEM] + [VMEM] * 8,
        out_specs=VMEM,
        compiler_params=PARAMS,
        name="post",
    )(core, mine, other_heads, pooled, members, w_out, gain_mlp.reshape(1, width), w_inner, w_outer)
    returned = lax.all_to_all(
        back.reshape(devices, tile, width), AXES, split_axis=0, concat_axis=0, tiled=True
    ).reshape(sen_dev, width)

    rows = math.gcd(sen_dev, 512)
    by_rows = pl.BlockSpec((rows, width), lambda i: (i, 0))
    whole = lambda shape: pl.BlockSpec(shape, lambda i: (0, 0))
    return pl.pallas_call(
        decode_kernel,
        grid=(sen_dev // rows,),
        out_shape=jax.ShapeDtypeStruct((sen_dev, width), BF16),
        in_specs=[
            by_rows,
            by_rows,
            pl.BlockSpec((rows, 1), lambda i: (i, 0)),
            whole((1, width)),
            whole(w_dec_in.shape),
            whole(w_dec_out.shape),
        ],
        out_specs=by_rows,
        compiler_params=PARAMS,
        name="decode",
    )(returned, sensors, live, gain_dec.reshape(1, width), w_dec_in, w_dec_out)


def solution(mesh):
    placed = (P(AXES, None), P(AXES)) + (P(),) * 12
    return jax.shard_map(
        local, mesh=mesh, in_specs=placed, out_specs=P(AXES, None), check_vma=False
    )
```

```python
import functools
import math

import jax
import jax.numpy as jnp
from jax import lax
from jax.experimental import pallas as pl
from jax.experimental.pallas import tpu as pltpu
from jax.sharding import PartitionSpec as P

HEADS = 8
HEAD_DIM = 64
KV_HEADS = 2
GROUP = HEADS // KV_HEADS
REG_DEV = 256
LANES = 128
EPS = 1e-06
AXES = ("seq", "dp")
F32 = jnp.float32
BF16 = jnp.bfloat16
NT = (((1,), (1,)), ((), ()))
TN = (((0,), (0,)), ((), ()))

VMEM = pl.BlockSpec(memory_space=pltpu.VMEM)
SMEM = pl.BlockSpec(memory_space=pltpu.SMEM)
PARAMS = pltpu.CompilerParams(vmem_limit_bytes=40 * 1024 * 1024)


def mm(a, b):
    return jnp.dot(a, b, preferred_element_type=F32)


def rms(values):
    return values * lax.rsqrt(jnp.mean(values * values, axis=-1, keepdims=True) + EPS)


def pack_kernel(tile, me_ref, sensors_ref, labels_ref, out_ref):
    per_row = LANES // tile
    blocks = sensors_ref.shape[1] // LANES
    tiles = out_ref.shape[0]
    mine = lax.rem(me_ref[0], per_row)
    labels = (labels_ref[...] + 1).astype(F32)
    lane = lax.broadcasted_iota(jnp.int32, labels.shape, 1)
    own_lanes = (lane // tile) == mine
    for k in range(per_row):
        shift = lax.rem(mine - k + per_row, per_row) * tile
        rolled = jnp.where(own_lanes, pltpu.roll(labels, shift, 1), 0.0)
        for g in range(tiles // per_row):
            t = g * per_row + k
            row = jnp.broadcast_to(rolled[g : g + 1, :], (8, LANES)).astype(BF16)
            rows = sensors_ref[t * tile : (t + 1) * tile, :]
            parts = [rows[:, c * LANES : (c + 1) * LANES] for c in range(blocks)]
            out_ref[t] = jnp.concatenate(parts + [row], axis=0)


def by_heads():
    at = lax.broadcasted_iota(jnp.int32, (LANES, LANES), 0) // HEAD_DIM
    to = lax.broadcasted_iota(jnp.int32, (LANES, LANES), 1) // HEAD_DIM
    return jnp.where(at == to, 1.0 / HEAD_DIM, 0.0).astype(BF16)


def low_lanes(rows):
    return lax.broadcasted_iota(jnp.int32, (rows, LANES), 1) < HEAD_DIM


def pool_kernel(
    tile, core_ref, got_ref, w_key_ref, w_value_ref, gain_ref, pooled_ref, member_ref, attn_in_ref, keep_ref, send_ref
):
    tiles, _, _ = got_ref.shape
    per_row = LANES // tile
    width = pooled_ref.shape[1]
    blocks = width // LANES
    slots = tiles * tile
    regions = lax.broadcasted_iota(jnp.int32, (REG_DEV, LANES), 0).astype(F32) + 1.0
    hits = jnp.zeros((REG_DEV, LANES), F32)
    for g in range(tiles // per_row):
        row = got_ref[g * per_row, tile * blocks : tile * blocks + 8, :].astype(F32)
        for k in range(1, per_row):
            row = row + got_ref[g * per_row + k, tile * blocks : tile * blocks + 8, :].astype(F32)
        hit = jnp.where(regions == row[0:1, :], 1.0, 0.0)
        hits = hits + hit
        member_ref[:, g * LANES : (g + 1) * LANES] = hit.astype(BF16)
    count = jnp.sum(hits, axis=1, keepdims=True)
    members = member_ref[...]
    sums = [
        mm(members, got_ref[:, c * tile : (c + 1) * tile, :].reshape(slots, LANES))
        for c in range(blocks)
    ]
    pooled = jnp.concatenate(sums, axis=1) * (1.0 / (1.0 + count))
    pooled_ref[...] = pooled
    attn_in = (rms(pooled) * gain_ref[...]).astype(BF16)
    attn_in_ref[...] = attn_in
    low = low_lanes(REG_DEV)
    key = mm(attn_in, w_key_ref[...])
    key = key * lax.rsqrt(mm((key * key).astype(BF16), by_heads()) + EPS)
    value = mm(attn_in, w_value_ref[...])
    zero = jnp.where(low, key, pltpu.roll(value, HEAD_DIM, 1)).astype(BF16)
    one = jnp.where(low, pltpu.roll(key, HEAD_DIM, 1), value).astype(BF16)
    first = core_ref[0] == 0
    keep_ref[...] = jnp.where(first, zero, one)
    send_ref[...] = jnp.where(first, one, zero)


def query_kernel(core_ref, attn_in_ref, w_query_ref, scale_ref, keep_ref, send_ref):
    core = core_ref[0]
    half = GROUP * HEAD_DIM
    low = low_lanes(REG_DEV)
    for out_ref, group in ((send_ref, 1 - core), (keep_ref, core)):
        cols = pl.ds(pl.multiple_of(group * half, half), half)
        query = mm(attn_in_ref[...], w_query_ref[:, cols])
        scale = scale_ref[:, cols]
        for j in range(half // LANES):
            pair = slice(j * LANES, (j + 1) * LANES)
            values = query[:, pair]
            square = mm((values * values).astype(BF16), by_heads())
            unit = values * lax.rsqrt(square + EPS) * scale[:, pair]
            even = jnp.where(low, unit, 0.0).astype(BF16)
            odd = jnp.where(low, pltpu.roll(unit, HEAD_DIM, 1), 0.0).astype(BF16)
            out_ref[:, 2 * j * LANES : (2 * j + 1) * LANES] = even
            out_ref[:, (2 * j + 1) * LANES : (2 * j + 2) * LANES] = odd


def attend_kernel(parts, row_parts, first, last, *refs):
    slabs, kvs = refs[: len(row_parts)], refs[len(row_parts) : len(row_parts) + parts]
    rest = refs[len(row_parts) + parts :]
    key_ref, value_ref, query_ref = rest[-3:]
    acc_in = None if first else rest[0]
    acc_ref = rest[-4]
    out_ref = rest[-5] if last else None
    rows_all = len(row_parts) * REG_DEV
    at = 0
    for kv_ref in kvs:
        kv = kv_ref[...]
        rows = kv.shape[0]
        key_ref[at : at + rows, :] = kv
        value_ref[at : at + rows, :] = jnp.where(low_lanes(rows), jnp.ones_like(kv), kv)
        at += rows
    for r, slab in enumerate(slabs):
        for h in range(GROUP):
            query_ref[h, r * REG_DEV : (r + 1) * REG_DEV, :] = slab[:, h * LANES : (h + 1) * LANES]
    block = max(n for n in range(REG_DEV, 2561, REG_DEV) if at % n == 0)
    span = min(rows_all, 512 if block <= 1024 else 256)

    def step(i, begin):
        keys = pl.ds(pl.multiple_of(i * block, block), block)
        for h in range(GROUP):
            for r in range(rows_all // span):
                here = slice(r * span, (r + 1) * span)
                score = lax.dot_general(
                    query_ref[h, here, :], key_ref[keys, :], NT, preferred_element_type=F32
                )
                new = mm(jnp.exp2(score).astype(BF16), value_ref[keys, :])
                if not begin:
                    new = acc_ref[h, here, :] + new
                elif not first:
                    base = row_parts[0] * REG_DEV
                    new = acc_in[h, base + r * span : base + (r + 1) * span, :] + new
                acc_ref[h, here, :] = new

    step(0, True)
    if at > block:

        def body(i, carry):
            step(i, False)
            return carry

        lax.fori_loop(1, at // block, body, 0)
    if last:
        low = low_lanes(rows_all)
        for j in range(GROUP // 2):
            a, b = acc_ref[2 * j], acc_ref[2 * j + 1]
            num = jnp.where(low, pltpu.roll(a, HEAD_DIM, 1), b)
            den = jnp.where(low, a, pltpu.roll(b, HEAD_DIM, 1))
            out_ref[:, j * LANES : (j + 1) * LANES] = (num / den).astype(BF16)


def post_kernel(
    core_ref, mine_ref, other_ref, pooled_ref, member_ref, w_out_ref, gain_ref, w_inner_ref, w_outer_ref, out_ref, inner_ref
):
    half = mine_ref.shape[1]
    core = core_ref[0]
    own = pl.ds(pl.multiple_of(core * half, half), half)
    far = pl.ds(pl.multiple_of((1 - core) * half, half), half)
    hidden = (
        pooled_ref[...] + mm(mine_ref[...], w_out_ref[own, :]) + mm(other_ref[...], w_out_ref[far, :])
    )
    mlp_in = (rms(hidden) * gain_ref[...]).astype(BF16)
    inner_width = w_inner_ref.shape[1]
    block = math.gcd(inner_width, 512)
    for j in range(inner_width // block):
        cols = slice(j * block, (j + 1) * block)
        inner_ref[:, cols] = jax.nn.gelu(mm(mlp_in, w_inner_ref[:, cols])).astype(BF16)
    region_out = (hidden + mm(inner_ref[...], w_outer_ref[...])).astype(BF16)
    slots = member_ref.shape[1]
    block = math.gcd(slots, 512)
    for i in range(slots // block):
        rows = slice(i * block, (i + 1) * block)
        out_ref[rows, :] = lax.dot_general(
            member_ref[:, rows], region_out, TN, preferred_element_type=F32
        ).astype(BF16)


def decode_kernel(back_ref, sensors_ref, live_ref, gain_ref, w_in_ref, w_out_ref, out_ref):
    count = out_ref.shape[0]
    block = math.gcd(count, 128)
    for i in range(count // block):
        rows = slice(i * block, (i + 1) * block)
        total = back_ref[rows, :].astype(F32) + sensors_ref[rows, :].astype(F32)
        dec_in = (rms(total) * gain_ref[...]).astype(BF16)
        hidden = jax.nn.gelu(mm(dec_in, w_in_ref[...])).astype(BF16)
        result = mm(hidden, w_out_ref[...])
        out_ref[rows, :] = jnp.where(live_ref[rows, :] > 0.0, result, 0.0).astype(BF16)


def local(
    sensors,
    slot_region,
    w_query,
    w_key,
    w_value,
    w_out,
    temper,
    gain_attn,
    w_inner,
    w_outer,
    gain_mlp,
    gain_dec,
    w_dec_in,
    w_dec_out,
):
    devices = lax.axis_size(AXES)
    sen_dev, width = sensors.shape
    tile = sen_dev // devices
    me = lax.axis_index(AXES).astype(jnp.int32).reshape(1)
    core = lax.rem(me, 2)
    bits = devices.bit_length() - 1
    pay_rows = tile * (width // LANES) + 8

    def flipped(value, mask):
        return lax.ppermute(value, AXES, [(i, i ^ mask) for i in range(devices)])

    payload = pl.pallas_call(
        functools.partial(pack_kernel, tile),
        out_shape=jax.ShapeDtypeStruct((devices, pay_rows, LANES), BF16),
        in_specs=[SMEM, VMEM, VMEM],
        out_specs=VMEM,
        compiler_params=PARAMS,
        name="pack",
    )(me, sensors, slot_region.reshape(-1, LANES))
    got = lax.all_to_all(payload, AXES, split_axis=0, concat_axis=0, tiled=True)

    scale = jnp.repeat(temper * (math.log2(math.e) / HEAD_DIM), HEAD_DIM).reshape(1, -1)
    live = (slot_region >= 0).astype(F32).reshape(sen_dev, 1)

    kv_shape = jax.ShapeDtypeStruct((REG_DEV, LANES), BF16)
    pooled, members, attn_in, kv_keep, kv_send = pl.pallas_call(
        functools.partial(pool_kernel, tile),
        out_shape=(
            jax.ShapeDtypeStruct((REG_DEV, width), F32),
            jax.ShapeDtypeStruct((REG_DEV, sen_dev), BF16),
            jax.ShapeDtypeStruct((REG_DEV, width), BF16),
            kv_shape,
            kv_shape,
        ),
        in_specs=[SMEM] + [VMEM] * 4,
        out_specs=(VMEM,) * 5,
        compiler_params=PARAMS,
        name="pool",
    )(core, got, w_key, w_value, gain_attn.reshape(1, width))
    kv_other = flipped(kv_send, 1)
    slab_shape = jax.ShapeDtypeStruct((REG_DEV, GROUP * LANES), BF16)
    q_keep, q_send = pl.pallas_call(
        query_kernel,
        out_shape=(slab_shape, slab_shape),
        in_specs=[SMEM] + [VMEM] * 3,
        out_specs=(VMEM, VMEM),
        compiler_params=PARAMS,
        cost_estimate=pl.CostEstimate(
            flops=2 * REG_DEV * width * width, bytes_accessed=2 * REG_DEV * width, transcendentals=0
        ),
        name="query",
    )(core, attn_in, w_query, scale)
    kv_other, q_keep, q_send = lax.optimization_barrier((kv_other, q_keep, q_send))
    slabs = (q_keep, flipped(q_send, 1))

    def attend(parts, acc, last=False, row_parts=(0, 1)):
        keys = sum(part.shape[0] for part in parts)
        rows = len(row_parts) * REG_DEV
        acc_shape = (GROUP, rows, LANES)
        work = GROUP * rows * keys
        out_shape = (rows, GROUP * HEAD_DIM) if last else acc_shape
        return pl.pallas_call(
            functools.partial(attend_kernel, len(parts), row_parts, acc is None, last),
            out_shape=jax.ShapeDtypeStruct(out_shape, BF16 if last else F32),
            in_specs=[VMEM] * (len(row_parts) + len(parts) + (acc is not None)),
            out_specs=VMEM,
            scratch_shapes=([pltpu.VMEM(acc_shape, F32)] if last else [])
            + [pltpu.VMEM((keys, LANES), BF16)] * 2
            + [pltpu.VMEM(acc_shape, BF16)],
            compiler_params=PARAMS,
            cost_estimate=pl.CostEstimate(
                flops=work * 4 * 256, bytes_accessed=keys * 2 * LANES, transcendentals=work
            ),
            name="attend",
        )(*(slabs[r] for r in row_parts), *parts, *(() if acc is None else (acc,)))

    one, two = 1 << (bits - 2), 1 << (bits - 1)
    own = jnp.concatenate([kv_keep, kv_other], axis=0)
    for bit in range(bits - 3, 2, -1):
        own = jnp.concatenate([own, flipped(own, 1 << bit)], axis=0)
    near, far = 1 << 1, 1 << 2

    a, b = flipped(own, far), flipped(own, near)
    own_one, own_two = flipped(own, one), flipped(own, two)
    acc = attend([own], None)
    acc, a, b, own_one, own_two = lax.optimization_barrier((acc, a, b, own_one, own_two))

    ab, c = jnp.concatenate([a, b], axis=0), flipped(a, near)
    ab_one, ab_two, own_corner = flipped(ab, one), flipped(ab, two), flipped(own_two, one)
    acc = attend([ab, own_one, own_two], acc)
    acc, c, ab_one, ab_two = lax.optimization_barrier((acc, c, ab_one, ab_two))

    c_one, c_two, ab_corner = flipped(c, one), flipped(c, two), flipped(ab_one, two)
    acc = attend([c, ab_one, ab_two, own_corner], acc)
    acc, c_one, c_two = lax.optimization_barrier((acc, c_one, c_two))

    c_corner = flipped(c_two, one)
    acc = attend([c_one, c_two, ab_corner], acc)

    theirs = attend([c_corner], acc, True, (1,))
    other_heads = flipped(theirs, 1)
    mine = attend([c_corner], acc, True, (0,))
    mine, other_heads = lax.optimization_barrier((mine, other_heads))

    back = pl.pallas_call(
        post_kernel,
        out_shape=jax.ShapeDtypeStruct((sen_dev, width), BF16),
        in_specs=[SMEM] + [VMEM] * 8,
        out_specs=VMEM,
        scratch_shapes=[pltpu.VMEM((REG_DEV, w_inner.shape[1]), BF16)],
        compiler_params=PARAMS,
        name="post",
    )(core, mine, other_heads, pooled, members, w_out, gain_mlp.reshape(1, width), w_inner, w_outer)
    returned = lax.all_to_all(
        back.reshape(devices, tile, width), AXES, split_axis=0, concat_axis=0, tiled=True
    ).reshape(sen_dev, width)

    rows = math.gcd(sen_dev, 512)
    by_rows = pl.BlockSpec((rows, width), lambda i: (i, 0))
    whole = lambda shape: pl.BlockSpec(shape, lambda i: (0, 0))
    return pl.pallas_call(
        decode_kernel,
        grid=(sen_dev // rows,),
        out_shape=jax.ShapeDtypeStruct((sen_dev, width), BF16),
        in_specs=[
            by_rows,
            by_rows,
            pl.BlockSpec((rows, 1), lambda i: (i, 0)),
            whole((1, width)),
            whole(w_dec_in.shape),
            whole(w_dec_out.shape),
        ],
        out_specs=by_rows,
        compiler_params=PARAMS,
        name="decode",
    )(returned, sensors, live, gain_dec.reshape(1, width), w_dec_in, w_dec_out)


def solution(mesh):
    placed = (P(AXES, None), P(AXES)) + (P(),) * 12
    return jax.shard_map(
        local, mesh=mesh, in_specs=placed, out_specs=P(AXES, None), check_vma=False
    )
```

```python
import functools
import math

import jax
import jax.numpy as jnp
from jax import lax
from jax.experimental import pallas as pl
from jax.experimental.pallas import tpu as pltpu
from jax.sharding import PartitionSpec as P

HEADS = 8
HEAD_DIM = 64
KV_HEADS = 2
GROUP = HEADS // KV_HEADS
REG_DEV = 256
LANES = 128
EPS = 1e-06
AXES = ("seq", "dp")
F32 = jnp.float32
BF16 = jnp.bfloat16
NT = (((1,), (1,)), ((), ()))
TN = (((0,), (0,)), ((), ()))

VMEM = pl.BlockSpec(memory_space=pltpu.VMEM)
SMEM = pl.BlockSpec(memory_space=pltpu.SMEM)
PARAMS = pltpu.CompilerParams(vmem_limit_bytes=40 * 1024 * 1024)


def mm(a, b):
    return jnp.dot(a, b, preferred_element_type=F32)


def rms(values):
    return values * lax.rsqrt(jnp.mean(values * values, axis=-1, keepdims=True) + EPS)


def pack_kernel(tile, me_ref, sensors_ref, labels_ref, out_ref):
    per_row = LANES // tile
    blocks = sensors_ref.shape[1] // LANES
    tiles = out_ref.shape[0]
    mine = lax.rem(me_ref[0], per_row)
    labels = (labels_ref[...] + 1).astype(F32)
    lane = lax.broadcasted_iota(jnp.int32, labels.shape, 1)
    own_lanes = (lane // tile) == mine
    for k in range(per_row):
        shift = lax.rem(mine - k + per_row, per_row) * tile
        rolled = jnp.where(own_lanes, pltpu.roll(labels, shift, 1), 0.0)
        for g in range(tiles // per_row):
            t = g * per_row + k
            row = jnp.broadcast_to(rolled[g : g + 1, :], (8, LANES)).astype(BF16)
            rows = sensors_ref[t * tile : (t + 1) * tile, :]
            parts = [rows[:, c * LANES : (c + 1) * LANES] for c in range(blocks)]
            out_ref[t] = jnp.concatenate(parts + [row], axis=0)


def by_heads():
    at = lax.broadcasted_iota(jnp.int32, (LANES, LANES), 0) // HEAD_DIM
    to = lax.broadcasted_iota(jnp.int32, (LANES, LANES), 1) // HEAD_DIM
    return jnp.where(at == to, 1.0 / HEAD_DIM, 0.0).astype(BF16)


def low_lanes(rows):
    return lax.broadcasted_iota(jnp.int32, (rows, LANES), 1) < HEAD_DIM


def pool_kernel(
    tile, core_ref, got_ref, w_key_ref, w_value_ref, gain_ref, pooled_ref, member_ref, attn_in_ref, keep_ref, send_ref
):
    tiles, _, _ = got_ref.shape
    per_row = LANES // tile
    width = pooled_ref.shape[1]
    blocks = width // LANES
    slots = tiles * tile
    regions = lax.broadcasted_iota(jnp.int32, (REG_DEV, LANES), 0).astype(F32) + 1.0
    hits = jnp.zeros((REG_DEV, LANES), F32)
    for g in range(tiles // per_row):
        row = got_ref[g * per_row, tile * blocks : tile * blocks + 8, :].astype(F32)
        for k in range(1, per_row):
            row = row + got_ref[g * per_row + k, tile * blocks : tile * blocks + 8, :].astype(F32)
        hit = jnp.where(regions == row[0:1, :], 1.0, 0.0)
        hits = hits + hit
        member_ref[:, g * LANES : (g + 1) * LANES] = hit.astype(BF16)
    count = jnp.sum(hits, axis=1, keepdims=True)
    members = member_ref[...]
    sums = [
        mm(members, got_ref[:, c * tile : (c + 1) * tile, :].reshape(slots, LANES))
        for c in range(blocks)
    ]
    pooled = jnp.concatenate(sums, axis=1) * (1.0 / (1.0 + count))
    pooled_ref[...] = pooled
    attn_in = (rms(pooled) * gain_ref[...]).astype(BF16)
    attn_in_ref[...] = attn_in
    low = low_lanes(REG_DEV)
    key = mm(attn_in, w_key_ref[...])
    key = key * lax.rsqrt(mm((key * key).astype(BF16), by_heads()) + EPS)
    value = mm(attn_in, w_value_ref[...])
    zero = jnp.where(low, key, pltpu.roll(value, HEAD_DIM, 1)).astype(BF16)
    one = jnp.where(low, pltpu.roll(key, HEAD_DIM, 1), value).astype(BF16)
    first = core_ref[0] == 0
    keep_ref[...] = jnp.where(first, zero, one)
    send_ref[...] = jnp.where(first, one, zero)


def query_kernel(core_ref, attn_in_ref, w_query_ref, scale_ref, keep_ref, send_ref):
    core = core_ref[0]
    half = GROUP * HEAD_DIM
    low = low_lanes(REG_DEV)
    for out_ref, group in ((send_ref, 1 - core), (keep_ref, core)):
        cols = pl.ds(pl.multiple_of(group * half, half), half)
        query = mm(attn_in_ref[...], w_query_ref[:, cols])
        scale = scale_ref[:, cols]
        for j in range(half // LANES):
            pair = slice(j * LANES, (j + 1) * LANES)
            values = query[:, pair]
            square = mm((values * values).astype(BF16), by_heads())
            unit = values * lax.rsqrt(square + EPS) * scale[:, pair]
            even = jnp.where(low, unit, 0.0).astype(BF16)
            odd = jnp.where(low, pltpu.roll(unit, HEAD_DIM, 1), 0.0).astype(BF16)
            out_ref[:, 2 * j * LANES : (2 * j + 1) * LANES] = even
            out_ref[:, (2 * j + 1) * LANES : (2 * j + 2) * LANES] = odd


def attend_kernel(parts, row_parts, first, last, *refs):
    slabs, kvs = refs[: len(row_parts)], refs[len(row_parts) : len(row_parts) + parts]
    rest = refs[len(row_parts) + parts :]
    key_ref, value_ref, query_ref = rest[-3:]
    acc_in = None if first else rest[0]
    acc_ref = rest[-4]
    out_ref = rest[-5] if last else None
    rows_all = len(row_parts) * REG_DEV
    at = 0
    for kv_ref in kvs:
        kv = kv_ref[...]
        rows = kv.shape[0]
        key_ref[at : at + rows, :] = kv
        value_ref[at : at + rows, :] = jnp.where(low_lanes(rows), jnp.ones_like(kv), kv)
        at += rows
    for r, slab in enumerate(slabs):
        for h in range(GROUP):
            query_ref[h, r * REG_DEV : (r + 1) * REG_DEV, :] = slab[:, h * LANES : (h + 1) * LANES]
    block = max(n for n in range(REG_DEV, 2561, REG_DEV) if at % n == 0)
    span = min(rows_all, 512 if block <= 1024 else 256)

    def step(i, begin):
        keys = pl.ds(pl.multiple_of(i * block, block), block)
        for h in range(GROUP):
            for r in range(rows_all // span):
                here = slice(r * span, (r + 1) * span)
                score = lax.dot_general(
                    query_ref[h, here, :], key_ref[keys, :], NT, preferred_element_type=F32
                )
                new = mm(jnp.exp2(score).astype(BF16), value_ref[keys, :])
                if not begin:
                    new = acc_ref[h, here, :] + new
                elif not first:
                    base = row_parts[0] * REG_DEV
                    new = acc_in[h, base + r * span : base + (r + 1) * span, :] + new
                acc_ref[h, here, :] = new

    step(0, True)
    if at > block:

        def body(i, carry):
            step(i, False)
            return carry

        lax.fori_loop(1, at // block, body, 0)
    if last:
        low = low_lanes(rows_all)
        for j in range(GROUP // 2):
            a, b = acc_ref[2 * j], acc_ref[2 * j + 1]
            num = jnp.where(low, pltpu.roll(a, HEAD_DIM, 1), b)
            den = jnp.where(low, a, pltpu.roll(b, HEAD_DIM, 1))
            out_ref[:, j * LANES : (j + 1) * LANES] = (num / den).astype(BF16)


def post_kernel(
    core_ref, mine_ref, other_ref, pooled_ref, member_ref, w_out_ref, gain_ref, w_inner_ref, w_outer_ref, out_ref, inner_ref
):
    half = mine_ref.shape[1]
    core = core_ref[0]
    own = pl.ds(pl.multiple_of(core * half, half), half)
    far = pl.ds(pl.multiple_of((1 - core) * half, half), half)
    hidden = (
        pooled_ref[...] + mm(mine_ref[...], w_out_ref[own, :]) + mm(other_ref[...], w_out_ref[far, :])
    )
    mlp_in = (rms(hidden) * gain_ref[...]).astype(BF16)
    inner_width = w_inner_ref.shape[1]
    block = math.gcd(inner_width, 512)
    for j in range(inner_width // block):
        cols = slice(j * block, (j + 1) * block)
        inner_ref[:, cols] = jax.nn.gelu(mm(mlp_in, w_inner_ref[:, cols])).astype(BF16)
    region_out = (hidden + mm(inner_ref[...], w_outer_ref[...])).astype(BF16)
    slots = member_ref.shape[1]
    block = math.gcd(slots, 512)
    for i in range(slots // block):
        rows = slice(i * block, (i + 1) * block)
        out_ref[rows, :] = lax.dot_general(
            member_ref[:, rows], region_out, TN, preferred_element_type=F32
        ).astype(BF16)


def decode_kernel(back_ref, sensors_ref, live_ref, gain_ref, w_in_ref, w_out_ref, out_ref):
    count = out_ref.shape[0]
    block = math.gcd(count, 512)
    for i in range(count // block):
        rows = slice(i * block, (i + 1) * block)
        total = back_ref[rows, :].astype(F32) + sensors_ref[rows, :].astype(F32)
        dec_in = (rms(total) * gain_ref[...]).astype(BF16)
        hidden = jax.nn.gelu(mm(dec_in, w_in_ref[...])).astype(BF16)
        result = mm(hidden, w_out_ref[...])
        out_ref[rows, :] = jnp.where(live_ref[rows, :] > 0.0, result, 0.0).astype(BF16)


def local(
    sensors,
    slot_region,
    w_query,
    w_key,
    w_value,
    w_out,
    temper,
    gain_attn,
    w_inner,
    w_outer,
    gain_mlp,
    gain_dec,
    w_dec_in,
    w_dec_out,
):
    devices = lax.axis_size(AXES)
    sen_dev, width = sensors.shape
    tile = sen_dev // devices
    me = lax.axis_index(AXES).astype(jnp.int32).reshape(1)
    core = lax.rem(me, 2)
    bits = devices.bit_length() - 1
    pay_rows = tile * (width // LANES) + 8

    def flipped(value, mask):
        return lax.ppermute(value, AXES, [(i, i ^ mask) for i in range(devices)])

    payload = pl.pallas_call(
        functools.partial(pack_kernel, tile),
        out_shape=jax.ShapeDtypeStruct((devices, pay_rows, LANES), BF16),
        in_specs=[SMEM, VMEM, VMEM],
        out_specs=VMEM,
        compiler_params=PARAMS,
        name="pack",
    )(me, sensors, slot_region.reshape(-1, LANES))
    got = lax.all_to_all(payload, AXES, split_axis=0, concat_axis=0, tiled=True)

    scale = jnp.repeat(temper * (math.log2(math.e) / HEAD_DIM), HEAD_DIM).reshape(1, -1)
    live = (slot_region >= 0).astype(F32).reshape(sen_dev, 1)

    kv_shape = jax.ShapeDtypeStruct((REG_DEV, LANES), BF16)
    pooled, members, attn_in, kv_keep, kv_send = pl.pallas_call(
        functools.partial(pool_kernel, tile),
        out_shape=(
            jax.ShapeDtypeStruct((REG_DEV, width), F32),
            jax.ShapeDtypeStruct((REG_DEV, sen_dev), BF16),
            jax.ShapeDtypeStruct((REG_DEV, width), BF16),
            kv_shape,
            kv_shape,
        ),
        in_specs=[SMEM] + [VMEM] * 4,
        out_specs=(VMEM,) * 5,
        compiler_params=PARAMS,
        name="pool",
    )(core, got, w_key, w_value, gain_attn.reshape(1, width))
    kv_other = flipped(kv_send, 1)
    slab_shape = jax.ShapeDtypeStruct((REG_DEV, GROUP * LANES), BF16)
    q_keep, q_send = pl.pallas_call(
        query_kernel,
        out_shape=(slab_shape, slab_shape),
        in_specs=[SMEM] + [VMEM] * 3,
        out_specs=(VMEM, VMEM),
        compiler_params=PARAMS,
        cost_estimate=pl.CostEstimate(
            flops=2 * REG_DEV * width * width, bytes_accessed=2 * REG_DEV * width, transcendentals=0
        ),
        name="query",
    )(core, attn_in, w_query, scale)
    kv_other, q_keep, q_send = lax.optimization_barrier((kv_other, q_keep, q_send))
    slabs = (q_keep, flipped(q_send, 1))

    def attend(parts, acc, last=False, row_parts=(0, 1)):
        keys = sum(part.shape[0] for part in parts)
        rows = len(row_parts) * REG_DEV
        acc_shape = (GROUP, rows, LANES)
        work = GROUP * rows * keys
        out_shape = (rows, GROUP * HEAD_DIM) if last else acc_shape
        return pl.pallas_call(
            functools.partial(attend_kernel, len(parts), row_parts, acc is None, last),
            out_shape=jax.ShapeDtypeStruct(out_shape, BF16 if last else F32),
            in_specs=[VMEM] * (len(row_parts) + len(parts) + (acc is not None)),
            out_specs=VMEM,
            scratch_shapes=([pltpu.VMEM(acc_shape, F32)] if last else [])
            + [pltpu.VMEM((keys, LANES), BF16)] * 2
            + [pltpu.VMEM(acc_shape, BF16)],
            compiler_params=PARAMS,
            cost_estimate=pl.CostEstimate(
                flops=work * 4 * 256, bytes_accessed=keys * 2 * LANES, transcendentals=work
            ),
            name="attend",
        )(*(slabs[r] for r in row_parts), *parts, *(() if acc is None else (acc,)))

    one, two = 1 << (bits - 2), 1 << (bits - 1)
    own = jnp.concatenate([kv_keep, kv_other], axis=0)
    for bit in range(bits - 3, 2, -1):
        own = jnp.concatenate([own, flipped(own, 1 << bit)], axis=0)
    near, far = 1 << 1, 1 << 2

    a, own_one, own_two = flipped(own, far), flipped(own, one), flipped(own, two)
    acc = attend([own], None)
    acc, a, own_one, own_two = lax.optimization_barrier((acc, a, own_one, own_two))

    bc = flipped(jnp.concatenate([own, a], axis=0), near)
    a_one, a_two, own_corner = flipped(a, one), flipped(a, two), flipped(own_two, one)
    acc = attend([a, own_one, own_two], acc)
    acc, bc, a_one, a_two = lax.optimization_barrier((acc, bc, a_one, a_two))

    bc_one, bc_two, a_corner = flipped(bc, one), flipped(bc, two), flipped(a_one, two)
    acc = attend([bc, a_one, a_two, own_corner], acc)
    acc, bc_one, bc_two = lax.optimization_barrier((acc, bc_one, bc_two))

    c_corner = flipped(bc_two, one)
    acc = attend([bc_one, bc_two, a_corner], acc)

    theirs = attend([c_corner], acc, True, (1,))
    other_heads = flipped(theirs, 1)
    mine = attend([c_corner], acc, True, (0,))
    mine, other_heads = lax.optimization_barrier((mine, other_heads))

    back = pl.pallas_call(
        post_kernel,
        out_shape=jax.ShapeDtypeStruct((sen_dev, width), BF16),
        in_specs=[SMEM] + [VMEM] * 8,
        out_specs=VMEM,
        scratch_shapes=[pltpu.VMEM((REG_DEV, w_inner.shape[1]), BF16)],
        compiler_params=PARAMS,
        name="post",
    )(core, mine, other_heads, pooled, members, w_out, gain_mlp.reshape(1, width), w_inner, w_outer)
    returned = lax.all_to_all(
        back.reshape(devices, tile, width), AXES, split_axis=0, concat_axis=0, tiled=True
    ).reshape(sen_dev, width)

    rows = math.gcd(sen_dev, 512)
    by_rows = pl.BlockSpec((rows, width), lambda i: (i, 0))
    whole = lambda shape: pl.BlockSpec(shape, lambda i: (0, 0))
    return pl.pallas_call(
        decode_kernel,
        grid=(sen_dev // rows,),
        out_shape=jax.ShapeDtypeStruct((sen_dev, width), BF16),
        in_specs=[
            by_rows,
            by_rows,
            pl.BlockSpec((rows, 1), lambda i: (i, 0)),
            whole((1, width)),
            whole(w_dec_in.shape),
            whole(w_dec_out.shape),
        ],
        out_specs=by_rows,
        compiler_params=PARAMS,
        name="decode",
    )(returned, sensors, live, gain_dec.reshape(1, width), w_dec_in, w_dec_out)


def solution(mesh):
    placed = (P(AXES, None), P(AXES)) + (P(),) * 12
    return jax.shard_map(
        local, mesh=mesh, in_specs=placed, out_specs=P(AXES, None), check_vma=False
    )
```

```python
import functools
import math

import jax
import jax.numpy as jnp
from jax import lax
from jax.experimental import pallas as pl
from jax.experimental.pallas import tpu as pltpu
from jax.sharding import PartitionSpec as P

HEADS = 8
HEAD_DIM = 64
KV_HEADS = 2
GROUP = HEADS // KV_HEADS
REG_DEV = 256
LANES = 128
EPS = 1e-06
AXIS = "device"
F32 = jnp.float32
BF16 = jnp.bfloat16
NT = (((1,), (1,)), ((), ()))
TN = (((0,), (0,)), ((), ()))

VMEM = pl.BlockSpec(memory_space=pltpu.VMEM)
SMEM = pl.BlockSpec(memory_space=pltpu.SMEM)
PARAMS = pltpu.CompilerParams(vmem_limit_bytes=40 * 1024 * 1024)


def mm(a, b):
    return jnp.dot(a, b, preferred_element_type=F32)


def rms(values):
    return values * lax.rsqrt(jnp.mean(values * values, axis=-1, keepdims=True) + EPS)


def pack_kernel(tile, order, place_ref, sensors_ref, labels_ref, out_ref):
    per_row = LANES // tile
    blocks = sensors_ref.shape[1] // LANES
    mine = lax.rem(place_ref[0], per_row)
    labels = (labels_ref[...] + 1).astype(F32)
    lane = lax.broadcasted_iota(jnp.int32, labels.shape, 1)
    own_lanes = (lane // tile) == mine
    for k in range(per_row):
        shift = lax.rem(mine - k + per_row, per_row) * tile
        rolled = jnp.where(own_lanes, pltpu.roll(labels, shift, 1), 0.0)
        for at, t in enumerate(order):
            if t % per_row != k:
                continue
            g = t // per_row
            row = jnp.broadcast_to(rolled[g : g + 1, :], (8, LANES)).astype(BF16)
            rows = sensors_ref[t * tile : (t + 1) * tile, :]
            parts = [rows[:, c * LANES : (c + 1) * LANES] for c in range(blocks)]
            out_ref[at] = jnp.concatenate(parts + [row], axis=0)


def by_heads():
    at = lax.broadcasted_iota(jnp.int32, (LANES, LANES), 0) // HEAD_DIM
    to = lax.broadcasted_iota(jnp.int32, (LANES, LANES), 1) // HEAD_DIM
    return jnp.where(at == to, 1.0 / HEAD_DIM, 0.0).astype(BF16)


def low_lanes(rows):
    return lax.broadcasted_iota(jnp.int32, (rows, LANES), 1) < HEAD_DIM


def pool_kernel(
    tile, core_ref, got_ref, w_key_ref, w_value_ref, gain_ref, pooled_ref, member_ref, attn_in_ref, keep_ref, send_ref
):
    tiles, _, _ = got_ref.shape
    per_row = LANES // tile
    width = pooled_ref.shape[1]
    blocks = width // LANES
    slots = tiles * tile
    regions = lax.broadcasted_iota(jnp.int32, (REG_DEV, LANES), 0).astype(F32) + 1.0
    hits = jnp.zeros((REG_DEV, LANES), F32)
    for g in range(tiles // per_row):
        row = got_ref[g * per_row, tile * blocks : tile * blocks + 8, :].astype(F32)
        for k in range(1, per_row):
            row = row + got_ref[g * per_row + k, tile * blocks : tile * blocks + 8, :].astype(F32)
        hit = jnp.where(regions == row[0:1, :], 1.0, 0.0)
        hits = hits + hit
        member_ref[:, g * LANES : (g + 1) * LANES] = hit.astype(BF16)
    count = jnp.sum(hits, axis=1, keepdims=True)
    members = member_ref[...]
    sums = [
        mm(members, got_ref[:, c * tile : (c + 1) * tile, :].reshape(slots, LANES))
        for c in range(blocks)
    ]
    pooled = jnp.concatenate(sums, axis=1) * (1.0 / (1.0 + count))
    pooled_ref[...] = pooled
    attn_in = (rms(pooled) * gain_ref[...]).astype(BF16)
    attn_in_ref[...] = attn_in
    low = low_lanes(REG_DEV)
    key = mm(attn_in, w_key_ref[...])
    key = key * lax.rsqrt(mm((key * key).astype(BF16), by_heads()) + EPS)
    value = mm(attn_in, w_value_ref[...])
    zero = jnp.where(low, key, pltpu.roll(value, HEAD_DIM, 1)).astype(BF16)
    one = jnp.where(low, pltpu.roll(key, HEAD_DIM, 1), value).astype(BF16)
    first = core_ref[0] == 0
    keep_ref[...] = jnp.where(first, zero, one)
    send_ref[...] = jnp.where(first, one, zero)


def query_kernel(core_ref, attn_in_ref, w_query_ref, scale_ref, keep_ref, send_ref):
    core = core_ref[0]
    half = GROUP * HEAD_DIM
    low = low_lanes(REG_DEV)
    for out_ref, group in ((send_ref, 1 - core), (keep_ref, core)):
        cols = pl.ds(pl.multiple_of(group * half, half), half)
        query = mm(attn_in_ref[...], w_query_ref[:, cols])
        scale = scale_ref[:, cols]
        for j in range(half // LANES):
            pair = slice(j * LANES, (j + 1) * LANES)
            values = query[:, pair]
            square = mm((values * values).astype(BF16), by_heads())
            unit = values * lax.rsqrt(square + EPS) * scale[:, pair]
            even = jnp.where(low, unit, 0.0).astype(BF16)
            odd = jnp.where(low, pltpu.roll(unit, HEAD_DIM, 1), 0.0).astype(BF16)
            out_ref[:, 2 * j * LANES : (2 * j + 1) * LANES] = even
            out_ref[:, (2 * j + 1) * LANES : (2 * j + 2) * LANES] = odd


def attend_kernel(parts, row_parts, first, last, *refs):
    slabs, kvs = refs[: len(row_parts)], refs[len(row_parts) : len(row_parts) + parts]
    rest = refs[len(row_parts) + parts :]
    key_ref, value_ref, query_ref = rest[-3:]
    acc_in = None if first else rest[0]
    acc_ref = rest[-4]
    out_ref = rest[-5] if last else None
    rows_all = len(row_parts) * REG_DEV
    at = 0
    for kv_ref in kvs:
        kv = kv_ref[...]
        rows = kv.shape[0]
        key_ref[at : at + rows, :] = kv
        value_ref[at : at + rows, :] = jnp.where(low_lanes(rows), jnp.ones_like(kv), kv)
        at += rows
    for r, slab in enumerate(slabs):
        for h in range(GROUP):
            query_ref[h, r * REG_DEV : (r + 1) * REG_DEV, :] = slab[:, h * LANES : (h + 1) * LANES]
    block = max(n for n in range(REG_DEV, 2561, REG_DEV) if at % n == 0)
    span = min(rows_all, 512 if block <= 1024 else 256)

    def step(i, begin):
        keys = pl.ds(pl.multiple_of(i * block, block), block)
        for h in range(GROUP):
            for r in range(rows_all // span):
                here = slice(r * span, (r + 1) * span)
                score = lax.dot_general(
                    query_ref[h, here, :], key_ref[keys, :], NT, preferred_element_type=F32
                )
                new = mm(jnp.exp2(score).astype(BF16), value_ref[keys, :])
                if not begin:
                    new = acc_ref[h, here, :] + new
                elif not first:
                    base = row_parts[0] * REG_DEV
                    new = acc_in[h, base + r * span : base + (r + 1) * span, :] + new
                acc_ref[h, here, :] = new

    step(0, True)
    if at > block:

        def body(i, carry):
            step(i, False)
            return carry

        lax.fori_loop(1, at // block, body, 0)
    if last:
        low = low_lanes(rows_all)
        for j in range(GROUP // 2):
            a, b = acc_ref[2 * j], acc_ref[2 * j + 1]
            num = jnp.where(low, pltpu.roll(a, HEAD_DIM, 1), b)
            den = jnp.where(low, a, pltpu.roll(b, HEAD_DIM, 1))
            out_ref[:, j * LANES : (j + 1) * LANES] = (num / den).astype(BF16)


def post_kernel(
    core_ref, mine_ref, other_ref, pooled_ref, member_ref, w_out_ref, gain_ref, w_inner_ref, w_outer_ref, out_ref, inner_ref
):
    half = mine_ref.shape[1]
    core = core_ref[0]
    own = pl.ds(pl.multiple_of(core * half, half), half)
    far = pl.ds(pl.multiple_of((1 - core) * half, half), half)
    hidden = (
        pooled_ref[...] + mm(mine_ref[...], w_out_ref[own, :]) + mm(other_ref[...], w_out_ref[far, :])
    )
    mlp_in = (rms(hidden) * gain_ref[...]).astype(BF16)
    inner_width = w_inner_ref.shape[1]
    block = math.gcd(inner_width, 512)
    for j in range(inner_width // block):
        cols = slice(j * block, (j + 1) * block)
        inner_ref[:, cols] = jax.nn.gelu(mm(mlp_in, w_inner_ref[:, cols])).astype(BF16)
    region_out = (hidden + mm(inner_ref[...], w_outer_ref[...])).astype(BF16)
    slots = member_ref.shape[1]
    block = math.gcd(slots, 512)
    for i in range(slots // block):
        rows = slice(i * block, (i + 1) * block)
        out_ref[rows, :] = lax.dot_general(
            member_ref[:, rows], region_out, TN, preferred_element_type=F32
        ).astype(BF16)


def decode_kernel(tile, order, back_ref, sensors_ref, live_ref, gain_ref, w_in_ref, w_out_ref, out_ref):
    step = min(len(order), 32)
    for begin in range(0, len(order), step):
        tiles = [slice(t * tile, (t + 1) * tile) for t in order[begin : begin + step]]
        sensors = jnp.concatenate([sensors_ref[rows, :] for rows in tiles], axis=0)
        back = back_ref[begin * tile : (begin + step) * tile, :]
        total = back.astype(F32) + sensors.astype(F32)
        dec_in = (rms(total) * gain_ref[...]).astype(BF16)
        hidden = jax.nn.gelu(mm(dec_in, w_in_ref[...])).astype(BF16)
        result = mm(hidden, w_out_ref[...])
        for i, rows in enumerate(tiles):
            here = result[i * tile : (i + 1) * tile, :]
            out_ref[rows, :] = jnp.where(live_ref[rows, :] > 0.0, here, 0.0).astype(BF16)


def local(
    order,
    sensors,
    slot_region,
    w_query,
    w_key,
    w_value,
    w_out,
    temper,
    gain_attn,
    w_inner,
    w_outer,
    gain_mlp,
    gain_dec,
    w_dec_in,
    w_dec_out,
):
    devices = len(order)
    sen_dev, width = sensors.shape
    tile = sen_dev // devices
    me = lax.axis_index(AXIS).astype(jnp.int32).reshape(1)
    core = lax.rem(me, 2)
    place = jnp.asarray([order.index(i) for i in range(devices)], jnp.int32)[me]
    bits = devices.bit_length() - 1
    pay_rows = tile * (width // LANES) + 8

    def flipped(value, mask):
        return lax.ppermute(value, AXIS, [(i, i ^ mask) for i in range(devices)])

    def exchanged(value):
        return lax.all_to_all(
            value, AXIS, split_axis=0, concat_axis=0, tiled=True, axis_index_groups=[order]
        )

    payload = pl.pallas_call(
        functools.partial(pack_kernel, tile, order),
        out_shape=jax.ShapeDtypeStruct((devices, pay_rows, LANES), BF16),
        in_specs=[SMEM, VMEM, VMEM],
        out_specs=VMEM,
        compiler_params=PARAMS,
        name="pack",
    )(place, sensors, slot_region.reshape(-1, LANES))
    got = exchanged(payload)

    scale = jnp.repeat(temper * (math.log2(math.e) / HEAD_DIM), HEAD_DIM).reshape(1, -1)
    live = (slot_region >= 0).astype(F32).reshape(sen_dev, 1)

    kv_shape = jax.ShapeDtypeStruct((REG_DEV, LANES), BF16)
    pooled, members, attn_in, kv_keep, kv_send = pl.pallas_call(
        functools.partial(pool_kernel, tile),
        out_shape=(
            jax.ShapeDtypeStruct((REG_DEV, width), F32),
            jax.ShapeDtypeStruct((REG_DEV, sen_dev), BF16),
            jax.ShapeDtypeStruct((REG_DEV, width), BF16),
            kv_shape,
            kv_shape,
        ),
        in_specs=[SMEM] + [VMEM] * 4,
        out_specs=(VMEM,) * 5,
        compiler_params=PARAMS,
        name="pool",
    )(core, got, w_key, w_value, gain_attn.reshape(1, width))
    kv_other = flipped(kv_send, 1)
    slab_shape = jax.ShapeDtypeStruct((REG_DEV, GROUP * LANES), BF16)
    q_keep, q_send = pl.pallas_call(
        query_kernel,
        out_shape=(slab_shape, slab_shape),
        in_specs=[SMEM] + [VMEM] * 3,
        out_specs=(VMEM, VMEM),
        compiler_params=PARAMS,
        cost_estimate=pl.CostEstimate(
            flops=2 * REG_DEV * width * width, bytes_accessed=2 * REG_DEV * width, transcendentals=0
        ),
        name="query",
    )(core, attn_in, w_query, scale)
    kv_other, q_keep, q_send = lax.optimization_barrier((kv_other, q_keep, q_send))
    slabs = (q_keep, flipped(q_send, 1))

    def attend(parts, acc, last=False, row_parts=(0, 1)):
        keys = sum(part.shape[0] for part in parts)
        rows = len(row_parts) * REG_DEV
        acc_shape = (GROUP, rows, LANES)
        work = GROUP * rows * keys
        out_shape = (rows, GROUP * HEAD_DIM) if last else acc_shape
        return pl.pallas_call(
            functools.partial(attend_kernel, len(parts), row_parts, acc is None, last),
            out_shape=jax.ShapeDtypeStruct(out_shape, BF16 if last else F32),
            in_specs=[VMEM] * (len(row_parts) + len(parts) + (acc is not None)),
            out_specs=VMEM,
            scratch_shapes=([pltpu.VMEM(acc_shape, F32)] if last else [])
            + [pltpu.VMEM((keys, LANES), BF16)] * 2
            + [pltpu.VMEM(acc_shape, BF16)],
            compiler_params=PARAMS,
            cost_estimate=pl.CostEstimate(
                flops=work * 4 * 256, bytes_accessed=keys * 2 * LANES, transcendentals=work
            ),
            name="attend",
        )(*(slabs[r] for r in row_parts), *parts, *(() if acc is None else (acc,)))

    one, two = 1 << (bits - 2), 1 << (bits - 1)
    own = jnp.concatenate([kv_keep, kv_other], axis=0)
    for bit in range(bits - 3, 2, -1):
        own = jnp.concatenate([own, flipped(own, 1 << bit)], axis=0)
    near, far = 1 << 1, 1 << 2

    hold = lax.optimization_barrier
    a, b = flipped(own, far), flipped(own, near)
    own_one, own_two = flipped(own, one), flipped(own, two)
    acc = attend([own], None)
    acc, own_one, own_two = hold((acc, own_one, own_two))
    acc = attend([own_one, own_two], acc)
    acc, a, b, own_two = hold((acc, a, b, own_two))

    ab, c = jnp.concatenate([a, b], axis=0), flipped(a, near)
    ab_one, ab_two, own_corner = flipped(ab, one), flipped(ab, two), flipped(own_two, one)
    acc = attend([ab], acc)
    acc, c, own_corner = hold((acc, c, own_corner))

    c_one, c_two = flipped(c, one), flipped(c, two)
    acc = attend([c, own_corner], acc)
    acc, ab_one, ab_two = hold((acc, ab_one, ab_two))

    ab_corner = flipped(ab_one, two)
    acc = attend([ab_one, ab_two], acc)
    acc, c_one, c_two = hold((acc, c_one, c_two))

    c_corner = flipped(c_two, one)
    acc = attend([c_one, c_two, ab_corner], acc)

    theirs = attend([c_corner], acc, True, (1,))
    other_heads = flipped(theirs, 1)
    mine = attend([c_corner], acc, True, (0,))
    mine, other_heads = lax.optimization_barrier((mine, other_heads))

    back = pl.pallas_call(
        post_kernel,
        out_shape=jax.ShapeDtypeStruct((sen_dev, width), BF16),
        in_specs=[SMEM] + [VMEM] * 8,
        out_specs=VMEM,
        scratch_shapes=[pltpu.VMEM((REG_DEV, w_inner.shape[1]), BF16)],
        compiler_params=PARAMS,
        name="post",
    )(core, mine, other_heads, pooled, members, w_out, gain_mlp.reshape(1, width), w_inner, w_outer)
    returned = exchanged(back.reshape(devices, tile, width)).reshape(sen_dev, width)
    return pl.pallas_call(
        functools.partial(decode_kernel, tile, order),
        out_shape=jax.ShapeDtypeStruct((sen_dev, width), BF16),
        in_specs=[VMEM] * 6,
        out_specs=VMEM,
        compiler_params=PARAMS,
        name="decode",
    )(returned, sensors, live, gain_dec.reshape(1, width), w_dec_in, w_dec_out)


def solution(mesh):
    devices, line = mesh.size, mesh.shape["dp"]
    order = sorted(range(devices), key=lambda i: (i // line, i % 2, i))
    flat = jax.sharding.Mesh(mesh.devices.reshape(-1), (AXIS,))
    placed = (P(AXIS, None), P(AXIS)) + (P(),) * 12
    return jax.shard_map(
        functools.partial(local, order),
        mesh=flat,
        in_specs=placed,
        out_specs=P(AXIS, None),
        check_vma=False,
    )
```

```python
import functools
import math

import jax
import jax.numpy as jnp
from jax import lax
from jax.experimental import pallas as pl
from jax.experimental.pallas import tpu as pltpu
from jax.sharding import PartitionSpec as P

HEADS = 8
HEAD_DIM = 64
KV_HEADS = 2
GROUP = HEADS // KV_HEADS
REG_DEV = 256
LANES = 128
EPS = 1e-06
AXIS = "device"
F32 = jnp.float32
BF16 = jnp.bfloat16
NT = (((1,), (1,)), ((), ()))
TN = (((0,), (0,)), ((), ()))

VMEM = pl.BlockSpec(memory_space=pltpu.VMEM)
SMEM = pl.BlockSpec(memory_space=pltpu.SMEM)
PARAMS = pltpu.CompilerParams(vmem_limit_bytes=40 * 1024 * 1024)


def mm(a, b):
    return jnp.dot(a, b, preferred_element_type=F32)


def rms(values):
    return values * lax.rsqrt(jnp.mean(values * values, axis=-1, keepdims=True) + EPS)


def pack_kernel(tile, order, place_ref, sensors_ref, labels_ref, out_ref):
    per_row = LANES // tile
    blocks = sensors_ref.shape[1] // LANES
    mine = lax.rem(place_ref[0], per_row)
    labels = (labels_ref[...] + 1).astype(F32)
    lane = lax.broadcasted_iota(jnp.int32, labels.shape, 1)
    own_lanes = (lane // tile) == mine
    rolled = []
    for k in range(per_row):
        shift = lax.rem(mine - k + per_row, per_row) * tile
        rolled.append(jnp.where(own_lanes, pltpu.roll(labels, shift, 1), 0.0))
    for at, t in enumerate(order):
        g = t // per_row
        row = jnp.broadcast_to(rolled[t % per_row][g : g + 1, :], (8, LANES)).astype(BF16)
        rows = sensors_ref[t * tile : (t + 1) * tile, :]
        parts = [rows[:, c * LANES : (c + 1) * LANES] for c in range(blocks)]
        out_ref[at] = jnp.concatenate(parts + [row], axis=0)


def by_heads():
    at = lax.broadcasted_iota(jnp.int32, (LANES, LANES), 0) // HEAD_DIM
    to = lax.broadcasted_iota(jnp.int32, (LANES, LANES), 1) // HEAD_DIM
    return jnp.where(at == to, 1.0 / HEAD_DIM, 0.0).astype(BF16)


def low_lanes(rows):
    return lax.broadcasted_iota(jnp.int32, (rows, LANES), 1) < HEAD_DIM


def pool_kernel(
    tile, core_ref, got_ref, w_key_ref, w_value_ref, gain_ref, pooled_ref, member_ref, attn_in_ref, keep_ref, send_ref
):
    tiles, _, _ = got_ref.shape
    per_row = LANES // tile
    width = pooled_ref.shape[1]
    blocks = width // LANES
    slots = tiles * tile
    regions = lax.broadcasted_iota(jnp.int32, (REG_DEV, LANES), 0).astype(F32) + 1.0
    hits = jnp.zeros((REG_DEV, LANES), F32)
    for g in range(tiles // per_row):
        row = got_ref[g * per_row, tile * blocks : tile * blocks + 8, :].astype(F32)
        for k in range(1, per_row):
            row = row + got_ref[g * per_row + k, tile * blocks : tile * blocks + 8, :].astype(F32)
        hit = jnp.where(regions == row[0:1, :], 1.0, 0.0)
        hits = hits + hit
        member_ref[:, g * LANES : (g + 1) * LANES] = hit.astype(BF16)
    count = jnp.sum(hits, axis=1, keepdims=True)
    members = member_ref[...]
    sums = [
        mm(members, got_ref[:, c * tile : (c + 1) * tile, :].reshape(slots, LANES))
        for c in range(blocks)
    ]
    pooled = jnp.concatenate(sums, axis=1) * (1.0 / (1.0 + count))
    pooled_ref[...] = pooled
    attn_in = (rms(pooled) * gain_ref[...]).astype(BF16)
    attn_in_ref[...] = attn_in
    low = low_lanes(REG_DEV)
    key = mm(attn_in, w_key_ref[...])
    key = key * lax.rsqrt(mm((key * key).astype(BF16), by_heads()) + EPS)
    value = mm(attn_in, w_value_ref[...])
    zero = jnp.where(low, key, pltpu.roll(value, HEAD_DIM, 1)).astype(BF16)
    one = jnp.where(low, pltpu.roll(key, HEAD_DIM, 1), value).astype(BF16)
    first = core_ref[0] == 0
    keep_ref[...] = jnp.where(first, zero, one)
    send_ref[...] = jnp.where(first, one, zero)


def query_kernel(core_ref, attn_in_ref, w_query_ref, scale_ref, keep_ref, send_ref):
    core = core_ref[0]
    half = GROUP * HEAD_DIM
    low = low_lanes(REG_DEV)
    for out_ref, group in ((send_ref, 1 - core), (keep_ref, core)):
        cols = pl.ds(pl.multiple_of(group * half, half), half)
        query = mm(attn_in_ref[...], w_query_ref[:, cols])
        scale = scale_ref[:, cols]
        for j in range(half // LANES):
            pair = slice(j * LANES, (j + 1) * LANES)
            values = query[:, pair]
            square = mm((values * values).astype(BF16), by_heads())
            unit = values * lax.rsqrt(square + EPS) * scale[:, pair]
            even = jnp.where(low, unit, 0.0).astype(BF16)
            odd = jnp.where(low, pltpu.roll(unit, HEAD_DIM, 1), 0.0).astype(BF16)
            out_ref[:, 2 * j * LANES : (2 * j + 1) * LANES] = even
            out_ref[:, (2 * j + 1) * LANES : (2 * j + 2) * LANES] = odd


def attend_kernel(parts, row_parts, first, last, *refs):
    slabs, kvs = refs[: len(row_parts)], refs[len(row_parts) : len(row_parts) + parts]
    rest = refs[len(row_parts) + parts :]
    key_ref, value_ref, query_ref = rest[-3:]
    acc_in = None if first else rest[0]
    acc_ref = rest[-4]
    out_ref = rest[-5] if last else None
    rows_all = len(row_parts) * REG_DEV
    at = 0
    for kv_ref in kvs:
        kv = kv_ref[...]
        rows = kv.shape[0]
        key_ref[at : at + rows, :] = kv
        value_ref[at : at + rows, :] = jnp.where(low_lanes(rows), jnp.ones_like(kv), kv)
        at += rows
    for r, slab in enumerate(slabs):
        for h in range(GROUP):
            query_ref[h, r * REG_DEV : (r + 1) * REG_DEV, :] = slab[:, h * LANES : (h + 1) * LANES]
    block = max(n for n in range(REG_DEV, 2561, REG_DEV) if at % n == 0)
    span = min(rows_all, 512 if block <= 1024 else 256)

    def step(i, begin):
        keys = pl.ds(pl.multiple_of(i * block, block), block)
        for h in range(GROUP):
            for r in range(rows_all // span):
                here = slice(r * span, (r + 1) * span)
                score = lax.dot_general(
                    query_ref[h, here, :], key_ref[keys, :], NT, preferred_element_type=F32
                )
                new = mm(jnp.exp2(score).astype(BF16), value_ref[keys, :])
                if not begin:
                    new = acc_ref[h, here, :] + new
                elif not first:
                    base = row_parts[0] * REG_DEV
                    new = acc_in[h, base + r * span : base + (r + 1) * span, :] + new
                acc_ref[h, here, :] = new

    step(0, True)
    if at > block:

        def body(i, carry):
            step(i, False)
            return carry

        lax.fori_loop(1, at // block, body, 0)
    if last:
        low = low_lanes(rows_all)
        for j in range(GROUP // 2):
            a, b = acc_ref[2 * j], acc_ref[2 * j + 1]
            num = jnp.where(low, pltpu.roll(a, HEAD_DIM, 1), b)
            den = jnp.where(low, a, pltpu.roll(b, HEAD_DIM, 1))
            out_ref[:, j * LANES : (j + 1) * LANES] = (num / den).astype(BF16)


def post_kernel(
    core_ref, mine_ref, other_ref, pooled_ref, member_ref, w_out_ref, gain_ref, w_inner_ref, w_outer_ref, out_ref, inner_ref
):
    half = mine_ref.shape[1]
    core = core_ref[0]
    own = pl.ds(pl.multiple_of(core * half, half), half)
    far = pl.ds(pl.multiple_of((1 - core) * half, half), half)
    hidden = (
        pooled_ref[...] + mm(mine_ref[...], w_out_ref[own, :]) + mm(other_ref[...], w_out_ref[far, :])
    )
    mlp_in = (rms(hidden) * gain_ref[...]).astype(BF16)
    inner_width = w_inner_ref.shape[1]
    block = math.gcd(inner_width, 512)
    for j in range(inner_width // block):
        cols = slice(j * block, (j + 1) * block)
        inner_ref[:, cols] = jax.nn.gelu(mm(mlp_in, w_inner_ref[:, cols])).astype(BF16)
    region_out = (hidden + mm(inner_ref[...], w_outer_ref[...])).astype(BF16)
    slots = member_ref.shape[1]
    block = math.gcd(slots, 512)
    for i in range(slots // block):
        rows = slice(i * block, (i + 1) * block)
        out_ref[rows, :] = lax.dot_general(
            member_ref[:, rows], region_out, TN, preferred_element_type=F32
        ).astype(BF16)


def decode_kernel(tile, order, back_ref, sensors_ref, live_ref, gain_ref, w_in_ref, w_out_ref, out_ref):
    step = min(len(order), 32)
    for begin in range(0, len(order), step):
        tiles = [slice(t * tile, (t + 1) * tile) for t in order[begin : begin + step]]
        sensors = jnp.concatenate([sensors_ref[rows, :] for rows in tiles], axis=0)
        back = back_ref[begin * tile : (begin + step) * tile, :]
        total = back.astype(F32) + sensors.astype(F32)
        dec_in = (rms(total) * gain_ref[...]).astype(BF16)
        hidden = jax.nn.gelu(mm(dec_in, w_in_ref[...])).astype(BF16)
        result = mm(hidden, w_out_ref[...])
        for i, rows in enumerate(tiles):
            here = result[i * tile : (i + 1) * tile, :]
            out_ref[rows, :] = jnp.where(live_ref[rows, :] > 0.0, here, 0.0).astype(BF16)


def local(
    order,
    line,
    sensors,
    slot_region,
    w_query,
    w_key,
    w_value,
    w_out,
    temper,
    gain_attn,
    w_inner,
    w_outer,
    gain_mlp,
    gain_dec,
    w_dec_in,
    w_dec_out,
):
    devices = len(order)
    sen_dev, width = sensors.shape
    tile = sen_dev // devices
    me = lax.axis_index(AXIS).astype(jnp.int32).reshape(1)
    core = lax.rem(me, 2)
    place = me // line * line + core * (line // 2) + me % line // 2
    bits = devices.bit_length() - 1
    pay_rows = tile * (width // LANES) + 8

    def flipped(value, mask):
        return lax.ppermute(value, AXIS, [(i, i ^ mask) for i in range(devices)])

    def exchanged(value):
        return lax.all_to_all(
            value, AXIS, split_axis=0, concat_axis=0, tiled=True, axis_index_groups=[order]
        )

    payload = pl.pallas_call(
        functools.partial(pack_kernel, tile, order),
        out_shape=jax.ShapeDtypeStruct((devices, pay_rows, LANES), BF16),
        in_specs=[SMEM, VMEM, VMEM],
        out_specs=VMEM,
        compiler_params=PARAMS,
        name="pack",
    )(place, sensors, slot_region.reshape(-1, LANES))
    got = exchanged(payload)

    scale = jnp.repeat(temper * (math.log2(math.e) / HEAD_DIM), HEAD_DIM).reshape(1, -1)
    live = (slot_region >= 0).astype(F32).reshape(sen_dev, 1)

    kv_shape = jax.ShapeDtypeStruct((REG_DEV, LANES), BF16)
    pooled, members, attn_in, kv_keep, kv_send = pl.pallas_call(
        functools.partial(pool_kernel, tile),
        out_shape=(
            jax.ShapeDtypeStruct((REG_DEV, width), F32),
            jax.ShapeDtypeStruct((REG_DEV, sen_dev), BF16),
            jax.ShapeDtypeStruct((REG_DEV, width), BF16),
            kv_shape,
            kv_shape,
        ),
        in_specs=[SMEM] + [VMEM] * 4,
        out_specs=(VMEM,) * 5,
        compiler_params=PARAMS,
        name="pool",
    )(core, got, w_key, w_value, gain_attn.reshape(1, width))
    kv_other = flipped(kv_send, 1)
    slab_shape = jax.ShapeDtypeStruct((REG_DEV, GROUP * LANES), BF16)
    q_keep, q_send = pl.pallas_call(
        query_kernel,
        out_shape=(slab_shape, slab_shape),
        in_specs=[SMEM] + [VMEM] * 3,
        out_specs=(VMEM, VMEM),
        compiler_params=PARAMS,
        cost_estimate=pl.CostEstimate(
            flops=2 * REG_DEV * width * width, bytes_accessed=2 * REG_DEV * width, transcendentals=0
        ),
        name="query",
    )(core, attn_in, w_query, scale)
    kv_other, q_keep, q_send = lax.optimization_barrier((kv_other, q_keep, q_send))
    slabs = (q_keep, flipped(q_send, 1))

    def attend(parts, acc, last=False, row_parts=(0, 1)):
        keys = sum(part.shape[0] for part in parts)
        rows = len(row_parts) * REG_DEV
        acc_shape = (GROUP, rows, LANES)
        work = GROUP * rows * keys
        out_shape = (rows, GROUP * HEAD_DIM) if last else acc_shape
        return pl.pallas_call(
            functools.partial(attend_kernel, len(parts), row_parts, acc is None, last),
            out_shape=jax.ShapeDtypeStruct(out_shape, BF16 if last else F32),
            in_specs=[VMEM] * (len(row_parts) + len(parts) + (acc is not None)),
            out_specs=VMEM,
            scratch_shapes=([pltpu.VMEM(acc_shape, F32)] if last else [])
            + [pltpu.VMEM((keys, LANES), BF16)] * 2
            + [pltpu.VMEM(acc_shape, BF16)],
            compiler_params=PARAMS,
            cost_estimate=pl.CostEstimate(
                flops=work * 4 * 256, bytes_accessed=keys * 2 * LANES, transcendentals=work
            ),
            name="attend",
        )(*(slabs[r] for r in row_parts), *parts, *(() if acc is None else (acc,)))

    one, two = 1 << (bits - 2), 1 << (bits - 1)
    own = jnp.concatenate([kv_keep, kv_other], axis=0)
    for bit in range(bits - 3, 2, -1):
        own = jnp.concatenate([own, flipped(own, 1 << bit)], axis=0)
    near, far = 1 << 1, 1 << 2

    hold = lax.optimization_barrier
    a, b = flipped(own, far), flipped(own, near)
    own_one, own_two = flipped(own, one), flipped(own, two)
    acc = attend([own], None)
    acc, own_one, own_two = hold((acc, own_one, own_two))
    own_corner = flipped(own_two, one)
    acc = attend([own_one, own_two], acc)
    acc, a, b = hold((acc, a, b))

    ab, c = jnp.concatenate([a, b], axis=0), flipped(a, near)
    ab_one, ab_two = flipped(ab, one), flipped(ab, two)
    acc = attend([ab], acc)
    acc, c, own_corner = hold((acc, c, own_corner))

    c_one, c_two = flipped(c, one), flipped(c, two)
    acc = attend([c, own_corner], acc)
    acc, ab_one, ab_two = hold((acc, ab_one, ab_two))

    ab_corner = flipped(ab_one, two)
    acc = attend([ab_one, ab_two], acc)
    acc, c_one, c_two = hold((acc, c_one, c_two))

    c_corner = flipped(c_two, one)
    acc = attend([c_one, c_two, ab_corner], acc)

    theirs = attend([c_corner], acc, True, (1,))
    other_heads = flipped(theirs, 1)
    mine = attend([c_corner], acc, True, (0,))
    mine, other_heads = lax.optimization_barrier((mine, other_heads))

    back = pl.pallas_call(
        post_kernel,
        out_shape=jax.ShapeDtypeStruct((sen_dev, width), BF16),
        in_specs=[SMEM] + [VMEM] * 8,
        out_specs=VMEM,
        scratch_shapes=[pltpu.VMEM((REG_DEV, w_inner.shape[1]), BF16)],
        compiler_params=PARAMS,
        name="post",
    )(core, mine, other_heads, pooled, members, w_out, gain_mlp.reshape(1, width), w_inner, w_outer)
    returned = exchanged(back.reshape(devices, tile, width)).reshape(sen_dev, width)
    return pl.pallas_call(
        functools.partial(decode_kernel, tile, order),
        out_shape=jax.ShapeDtypeStruct((sen_dev, width), BF16),
        in_specs=[VMEM] * 6,
        out_specs=VMEM,
        compiler_params=PARAMS,
        name="decode",
    )(returned, sensors, live, gain_dec.reshape(1, width), w_dec_in, w_dec_out)


def solution(mesh):
    devices, line = mesh.size, mesh.shape["dp"]
    order = sorted(range(devices), key=lambda i: (i // line, i % 2, i))
    flat = jax.sharding.Mesh(mesh.devices.reshape(-1), (AXIS,))
    placed = (P(AXIS, None), P(AXIS)) + (P(),) * 12
    return jax.shard_map(
        functools.partial(local, order, line),
        mesh=flat,
        in_specs=placed,
        out_specs=P(AXIS, None),
        check_vma=False,
    )
```

```python
import functools
import math

import jax
import jax.numpy as jnp
from jax import lax
from jax.experimental import pallas as pl
from jax.experimental.pallas import tpu as pltpu
from jax.sharding import PartitionSpec as P

HEADS = 8
HEAD_DIM = 64
KV_HEADS = 2
GROUP = HEADS // KV_HEADS
REG_DEV = 256
LANES = 128
EPS = 1e-06
AXIS = "device"
F32 = jnp.float32
BF16 = jnp.bfloat16
NT = (((1,), (1,)), ((), ()))
TN = (((0,), (0,)), ((), ()))

VMEM = pl.BlockSpec(memory_space=pltpu.VMEM)
SMEM = pl.BlockSpec(memory_space=pltpu.SMEM)
HBM = pl.BlockSpec(memory_space=pltpu.HBM)
PARAMS = pltpu.CompilerParams(vmem_limit_bytes=40 * 1024 * 1024)


def mm(a, b):
    return jnp.dot(a, b, preferred_element_type=F32)


def gelu(values):
    half = 0.5 * values
    slope = math.sqrt(2.0 / math.pi)
    return half + half * jnp.tanh(values * (slope + slope * 0.044715 * values * values))


def rms(values):
    return values * lax.rsqrt(jnp.mean(values * values, axis=-1, keepdims=True) + EPS)


def pack_kernel(tile, order, place_ref, sensors_ref, labels_ref, out_ref, rows_ref, own_ref, sems):
    per_row = LANES // tile
    blocks = sensors_ref.shape[1] // LANES
    pieces = sems.shape[0] - 1
    piece = sensors_ref.shape[0] // pieces
    label_copy = pltpu.make_async_copy(labels_ref, own_ref, sems.at[pieces])
    label_copy.start()
    copies = []
    for i in range(pieces):
        here = slice(i * piece, (i + 1) * piece)
        copies.append(pltpu.make_async_copy(sensors_ref.at[here], rows_ref.at[here], sems.at[i]))
        copies[i].start()
    label_copy.wait()
    mine = lax.rem(place_ref[0], per_row)
    labels = (own_ref[...] + 1).astype(F32)
    lane = lax.broadcasted_iota(jnp.int32, labels.shape, 1)
    own_lanes = (lane // tile) == mine
    rolled = []
    for k in range(per_row):
        shift = lax.rem(mine - k + per_row, per_row) * tile
        rolled.append(jnp.where(own_lanes, pltpu.roll(labels, shift, 1), 0.0))
    for t in range(len(order)):
        if t * tile % piece == 0:
            copies[t * tile // piece].wait()
        g = t // per_row
        row = jnp.broadcast_to(rolled[t % per_row][g : g + 1, :], (8, LANES)).astype(BF16)
        rows = rows_ref[t * tile : (t + 1) * tile, :]
        parts = [rows[:, c * LANES : (c + 1) * LANES] for c in range(blocks)]
        out_ref[order.index(t)] = jnp.concatenate(parts + [row], axis=0)


def by_heads():
    at = lax.broadcasted_iota(jnp.int32, (LANES, LANES), 0) // HEAD_DIM
    to = lax.broadcasted_iota(jnp.int32, (LANES, LANES), 1) // HEAD_DIM
    return jnp.where(at == to, 1.0 / HEAD_DIM, 0.0).astype(BF16)


def low_lanes(rows):
    return lax.broadcasted_iota(jnp.int32, (rows, LANES), 1) < HEAD_DIM


def pool_kernel(
    tile, group_ref, got_ref, w_key_ref, w_value_ref, gain_ref, pooled_ref, member_ref, attn_in_ref, keep_ref, send_ref
):
    tiles, _, _ = got_ref.shape
    per_row = LANES // tile
    width = pooled_ref.shape[1]
    blocks = width // LANES
    slots = tiles * tile
    regions = lax.broadcasted_iota(jnp.int32, (REG_DEV, LANES), 0).astype(F32) + 1.0
    hits = jnp.zeros((REG_DEV, LANES), F32)
    for g in range(tiles // per_row):
        row = got_ref[g * per_row, tile * blocks : tile * blocks + 8, :].astype(F32)
        for k in range(1, per_row):
            row = row + got_ref[g * per_row + k, tile * blocks : tile * blocks + 8, :].astype(F32)
        hit = jnp.where(regions == row[0:1, :], 1.0, 0.0)
        hits = hits + hit
        member_ref[:, g * LANES : (g + 1) * LANES] = hit.astype(BF16)
    count = jnp.sum(hits, axis=1, keepdims=True)
    members = member_ref[...]
    sums = [
        mm(members, got_ref[:, c * tile : (c + 1) * tile, :].reshape(slots, LANES))
        for c in range(blocks)
    ]
    pooled = jnp.concatenate(sums, axis=1) * (1.0 / (1.0 + count))
    pooled_ref[...] = pooled
    attn_in = (rms(pooled) * gain_ref[...]).astype(BF16)
    attn_in_ref[...] = attn_in
    low = low_lanes(REG_DEV)
    key = mm(attn_in, w_key_ref[...])
    key = key * lax.rsqrt(mm((key * key).astype(BF16), by_heads()) + EPS)
    value = mm(attn_in, w_value_ref[...])
    zero = jnp.where(low, key, pltpu.roll(value, HEAD_DIM, 1)).astype(BF16)
    one = jnp.where(low, pltpu.roll(key, HEAD_DIM, 1), value).astype(BF16)
    first = group_ref[0] == 0
    keep_ref[...] = jnp.where(first, zero, one)
    send_ref[...] = jnp.where(first, one, zero)


def query_kernel(group_ref, attn_in_ref, w_query_ref, scale_ref, keep_ref, send_ref):
    mine = group_ref[0]
    half = GROUP * HEAD_DIM
    low = low_lanes(REG_DEV)
    for out_ref, group in ((send_ref, 1 - mine), (keep_ref, mine)):
        cols = pl.ds(pl.multiple_of(group * half, half), half)
        query = mm(attn_in_ref[...], w_query_ref[:, cols])
        scale = scale_ref[:, cols]
        for j in range(half // LANES):
            pair = slice(j * LANES, (j + 1) * LANES)
            values = query[:, pair]
            square = mm((values * values).astype(BF16), by_heads())
            unit = values * lax.rsqrt(square + EPS) * scale[:, pair]
            even = jnp.where(low, unit, 0.0).astype(BF16)
            odd = jnp.where(low, pltpu.roll(unit, HEAD_DIM, 1), 0.0).astype(BF16)
            out_ref[:, 2 * j * LANES : (2 * j + 1) * LANES] = even
            out_ref[:, (2 * j + 1) * LANES : (2 * j + 2) * LANES] = odd


def attend_kernel(parts, row_parts, first, last, *refs):
    slabs, kvs = refs[: len(row_parts)], refs[len(row_parts) : len(row_parts) + parts]
    rest = refs[len(row_parts) + parts :]
    key_ref, value_ref, query_ref = rest[-3:]
    acc_in = None if first else rest[0]
    acc_ref = rest[-4]
    out_ref = rest[-5] if last else None
    rows_all = len(row_parts) * REG_DEV
    at = 0
    for kv_ref in kvs:
        kv = kv_ref[...]
        rows = kv.shape[0]
        key_ref[at : at + rows, :] = kv
        value_ref[at : at + rows, :] = jnp.where(low_lanes(rows), jnp.ones_like(kv), kv)
        at += rows
    for r, slab in enumerate(slabs):
        for h in range(GROUP):
            query_ref[h, r * REG_DEV : (r + 1) * REG_DEV, :] = slab[:, h * LANES : (h + 1) * LANES]
    block = max(n for n in range(REG_DEV, 2561, REG_DEV) if at % n == 0)
    span = min(rows_all, 512 if block <= 1024 else 256)

    def step(i, begin):
        keys = pl.ds(pl.multiple_of(i * block, block), block)
        for h in range(GROUP):
            for r in range(rows_all // span):
                here = slice(r * span, (r + 1) * span)
                score = lax.dot_general(
                    query_ref[h, here, :], key_ref[keys, :], NT, preferred_element_type=F32
                )
                new = mm(jnp.exp2(score).astype(BF16), value_ref[keys, :])
                if not begin:
                    new = acc_ref[h, here, :] + new
                elif not first:
                    base = row_parts[0] * REG_DEV if acc_in.shape[1] > rows_all else 0
                    new = acc_in[h, base + r * span : base + (r + 1) * span, :] + new
                acc_ref[h, here, :] = new

    step(0, True)
    if at > block:

        def body(i, carry):
            step(i, False)
            return carry

        lax.fori_loop(1, at // block, body, 0)
    if last:
        low = low_lanes(rows_all)
        for j in range(GROUP // 2):
            a, b = acc_ref[2 * j], acc_ref[2 * j + 1]
            num = jnp.where(low, pltpu.roll(a, HEAD_DIM, 1), b)
            den = jnp.where(low, a, pltpu.roll(b, HEAD_DIM, 1))
            out_ref[:, j * LANES : (j + 1) * LANES] = (num / den).astype(BF16)


def post_kernel(
    group_ref, mine_ref, other_ref, pooled_ref, member_ref, w_out_ref, gain_ref, w_inner_ref, w_outer_ref, out_ref, inner_ref
):
    half = mine_ref.shape[1]
    group = group_ref[0]
    own = pl.ds(pl.multiple_of(group * half, half), half)
    far = pl.ds(pl.multiple_of((1 - group) * half, half), half)
    hidden = (
        pooled_ref[...] + mm(mine_ref[...], w_out_ref[own, :]) + mm(other_ref[...], w_out_ref[far, :])
    )
    mlp_in = (rms(hidden) * gain_ref[...]).astype(BF16)
    inner_width = w_inner_ref.shape[1]
    block = math.gcd(inner_width, 512)
    for j in range(inner_width // block):
        cols = slice(j * block, (j + 1) * block)
        inner_ref[:, cols] = gelu(mm(mlp_in, w_inner_ref[:, cols])).astype(BF16)
    region_out = (hidden + mm(inner_ref[...], w_outer_ref[...])).astype(BF16)
    slots = member_ref.shape[1]
    block = math.gcd(slots, 512)
    for i in range(slots // block):
        rows = slice(i * block, (i + 1) * block)
        out_ref[rows, :] = lax.dot_general(
            member_ref[:, rows], region_out, TN, preferred_element_type=F32
        ).astype(BF16)


def decode_kernel(tile, order, back_ref, sensors_ref, live_ref, gain_ref, w_in_ref, w_out_ref, out_ref):
    step = min(len(order), 32)
    for begin in range(0, len(order), step):
        tiles = [slice(t * tile, (t + 1) * tile) for t in order[begin : begin + step]]
        sensors = jnp.concatenate([sensors_ref[rows, :] for rows in tiles], axis=0)
        back = back_ref[begin * tile : (begin + step) * tile, :]
        total = back.astype(F32) + sensors.astype(F32)
        dec_in = (rms(total) * gain_ref[...]).astype(BF16)
        hidden = gelu(mm(dec_in, w_in_ref[...])).astype(BF16)
        result = mm(hidden, w_out_ref[...])
        for i, rows in enumerate(tiles):
            here = result[i * tile : (i + 1) * tile, :]
            out_ref[rows, :] = jnp.where(live_ref[rows, :] > 0.0, here, 0.0).astype(BF16)


def local(
    order,
    line,
    sensors,
    slot_region,
    w_query,
    w_key,
    w_value,
    w_out,
    temper,
    gain_attn,
    w_inner,
    w_outer,
    gain_mlp,
    gain_dec,
    w_dec_in,
    w_dec_out,
):
    devices = len(order)
    sen_dev, width = sensors.shape
    tile = sen_dev // devices
    me = lax.axis_index(AXIS).astype(jnp.int32).reshape(1)
    core = lax.rem(me, 2)
    place = me // line * line + core * (line // 2) + me % line // 2
    bits = devices.bit_length() - 1
    one, two = 1 << (bits - 2), 1 << (bits - 1)
    group = me // one % 2
    pay_rows = tile * (width // LANES) + 8

    def flipped(value, mask):
        return lax.ppermute(value, AXIS, [(i, i ^ mask) for i in range(devices)])

    def exchanged(value):
        return lax.all_to_all(
            value, AXIS, split_axis=0, concat_axis=0, tiled=True, axis_index_groups=[order]
        )

    payload = pl.pallas_call(
        functools.partial(pack_kernel, tile, order),
        out_shape=jax.ShapeDtypeStruct((devices, pay_rows, LANES), BF16),
        in_specs=[SMEM, HBM, HBM],
        out_specs=VMEM,
        scratch_shapes=[
            pltpu.VMEM(sensors.shape, BF16),
            pltpu.VMEM((sen_dev // LANES, LANES), jnp.int32),
            pltpu.SemaphoreType.DMA((5,)),
        ],
        compiler_params=PARAMS,
        name="pack",
    )(place, sensors, slot_region.reshape(-1, LANES))
    got = exchanged(payload)

    scale = jnp.repeat(temper * (math.log2(math.e) / HEAD_DIM), HEAD_DIM).reshape(1, -1)
    live = (slot_region >= 0).astype(F32).reshape(sen_dev, 1)

    kv_shape = jax.ShapeDtypeStruct((REG_DEV, LANES), BF16)
    pooled, members, attn_in, kv_keep, kv_send = pl.pallas_call(
        functools.partial(pool_kernel, tile),
        out_shape=(
            jax.ShapeDtypeStruct((REG_DEV, width), F32),
            jax.ShapeDtypeStruct((REG_DEV, sen_dev), BF16),
            jax.ShapeDtypeStruct((REG_DEV, width), BF16),
            kv_shape,
            kv_shape,
        ),
        in_specs=[SMEM] + [VMEM] * 4,
        out_specs=(VMEM,) * 5,
        compiler_params=PARAMS,
        name="pool",
    )(group, got, w_key, w_value, gain_attn.reshape(1, width))
    kv_other = flipped(kv_send, one)
    slab_shape = jax.ShapeDtypeStruct((REG_DEV, GROUP * LANES), BF16)
    q_keep, q_send = pl.pallas_call(
        query_kernel,
        out_shape=(slab_shape, slab_shape),
        in_specs=[SMEM] + [VMEM] * 3,
        out_specs=(VMEM, VMEM),
        compiler_params=PARAMS,
        cost_estimate=pl.CostEstimate(
            flops=2 * REG_DEV * width * width, bytes_accessed=2 * REG_DEV * width, transcendentals=0
        ),
        name="query",
    )(group, attn_in, w_query, scale)
    kv_other, q_keep, q_send = lax.optimization_barrier((kv_other, q_keep, q_send))
    slabs = (q_keep, flipped(q_send, one))

    def attend(parts, acc, last=False, row_parts=(0, 1)):
        keys = sum(part.shape[0] for part in parts)
        rows = len(row_parts) * REG_DEV
        acc_shape = (GROUP, rows, LANES)
        work = GROUP * rows * keys
        out_shape = (rows, GROUP * HEAD_DIM) if last else acc_shape
        return pl.pallas_call(
            functools.partial(attend_kernel, len(parts), row_parts, acc is None, last),
            out_shape=jax.ShapeDtypeStruct(out_shape, BF16 if last else F32),
            in_specs=[VMEM] * (len(row_parts) + len(parts) + (acc is not None)),
            out_specs=VMEM,
            scratch_shapes=([pltpu.VMEM(acc_shape, F32)] if last else [])
            + [pltpu.VMEM((keys, LANES), BF16)] * 2
            + [pltpu.VMEM(acc_shape, BF16)],
            compiler_params=PARAMS,
            cost_estimate=pl.CostEstimate(
                flops=work * 4 * 256, bytes_accessed=keys * 2 * LANES, transcendentals=work
            ),
            name="attend",
        )(*(slabs[r] for r in row_parts), *parts, *(() if acc is None else (acc,)))

    own = jnp.concatenate([kv_keep, kv_other], axis=0)
    for bit in range(bits - 3, 2, -1):
        own = jnp.concatenate([own, flipped(own, 1 << bit)], axis=0)
    near, far = 1 << 1, 1 << 2

    hold = lax.optimization_barrier
    a, b = flipped(own, far), flipped(own, near)
    own_two, own_core = flipped(own, two), flipped(own, 1)
    acc = attend([own], None)
    own_both = flipped(own_two, 1)
    acc = attend([own_core, own_two], acc)
    acc, a, b = hold((acc, a, b))

    ab, c = jnp.concatenate([a, b], axis=0), flipped(a, near)
    ab_two, ab_core = flipped(ab, two), flipped(ab, 1)
    acc = attend([ab, own_both], acc)
    acc, c = hold((acc, c))

    c_two, c_core = flipped(c, two), flipped(c, 1)
    acc = attend([c, ab_core], acc)
    acc, ab_two = hold((acc, ab_two))

    ab_both = flipped(ab_two, 1)
    acc = attend([ab_two, c_core], acc)
    acc, ab_both, c_two = hold((acc, ab_both, c_two))

    c_both = flipped(c_two, 1)
    partial = attend([ab_both, c_two], acc, False, (1,))
    theirs = attend([c_both], partial, True, (1,))
    other_heads = flipped(theirs, one)
    mine = attend([ab_both, c_two, c_both], acc, True, (0,))
    mine, other_heads = hold((mine, other_heads))

    back = pl.pallas_call(
        post_kernel,
        out_shape=jax.ShapeDtypeStruct((sen_dev, width), BF16),
        in_specs=[SMEM] + [VMEM] * 8,
        out_specs=VMEM,
        scratch_shapes=[pltpu.VMEM((REG_DEV, w_inner.shape[1]), BF16)],
        compiler_params=PARAMS,
        name="post",
    )(group, mine, other_heads, pooled, members, w_out, gain_mlp.reshape(1, width), w_inner, w_outer)
    returned = exchanged(back.reshape(devices, tile, width)).reshape(sen_dev, width)
    return pl.pallas_call(
        functools.partial(decode_kernel, tile, order),
        out_shape=jax.ShapeDtypeStruct((sen_dev, width), BF16),
        in_specs=[VMEM] * 6,
        out_specs=VMEM,
        compiler_params=PARAMS,
        name="decode",
    )(returned, sensors, live, gain_dec.reshape(1, width), w_dec_in, w_dec_out)


def solution(mesh):
    devices, line = mesh.size, mesh.shape["dp"]
    order = sorted(range(devices), key=lambda i: (i // line, i % 2, i))
    flat = jax.sharding.Mesh(mesh.devices.reshape(-1), (AXIS,))
    placed = (P(AXIS, None), P(AXIS)) + (P(),) * 12
    return jax.shard_map(
        functools.partial(local, order, line),
        mesh=flat,
        in_specs=placed,
        out_specs=P(AXIS, None),
        check_vma=False,
    )
```

```python
import functools
import math

import jax
import jax.numpy as jnp
from jax import lax
from jax.experimental import pallas as pl
from jax.experimental.pallas import tpu as pltpu
from jax.sharding import PartitionSpec as P

HEADS = 8
HEAD_DIM = 64
KV_HEADS = 2
GROUP = HEADS // KV_HEADS
REG_DEV = 256
LANES = 128
EPS = 1e-06
AXIS = "device"
F32 = jnp.float32
BF16 = jnp.bfloat16
NT = (((1,), (1,)), ((), ()))
TN = (((0,), (0,)), ((), ()))

VMEM = pl.BlockSpec(memory_space=pltpu.VMEM)
SMEM = pl.BlockSpec(memory_space=pltpu.SMEM)
PARAMS = pltpu.CompilerParams(vmem_limit_bytes=40 * 1024 * 1024)


def mm(a, b):
    return jnp.dot(a, b, preferred_element_type=F32)


def gelu(values):
    half = 0.5 * values
    slope = math.sqrt(2.0 / math.pi)
    return half + half * jnp.tanh(values * (slope + slope * 0.044715 * values * values))


def rms(values):
    return values * lax.rsqrt(jnp.mean(values * values, axis=-1, keepdims=True) + EPS)


def pack_kernel(tile, order, place_ref, sensors_ref, labels_ref, out_ref):
    per_row = LANES // tile
    blocks = sensors_ref.shape[1] // LANES
    mine = lax.rem(place_ref[0], per_row)
    labels = labels_ref[...]
    lane = lax.broadcasted_iota(jnp.int32, labels.shape, 1)
    own_lanes = (lane // tile) == mine
    rolled = []
    for k in range(per_row):
        shift = lax.rem(mine - k + per_row, per_row) * tile
        rolled.append(jnp.where(own_lanes, pltpu.roll(labels, shift, 1), 0.0))
    for at, t in enumerate(order):
        g = t // per_row
        row = jnp.broadcast_to(rolled[t % per_row][g : g + 1, :], (8, LANES)).astype(BF16)
        rows = sensors_ref[t * tile : (t + 1) * tile, :]
        parts = [rows[:, c * LANES : (c + 1) * LANES] for c in range(blocks)]
        out_ref[at] = jnp.concatenate(parts + [row], axis=0)


def by_heads():
    at = lax.broadcasted_iota(jnp.int32, (LANES, LANES), 0) // HEAD_DIM
    to = lax.broadcasted_iota(jnp.int32, (LANES, LANES), 1) // HEAD_DIM
    return jnp.where(at == to, 1.0 / HEAD_DIM, 0.0).astype(BF16)


def low_lanes(rows):
    return lax.broadcasted_iota(jnp.int32, (rows, LANES), 1) < HEAD_DIM


def pool_kernel(
    tile, group_ref, got_ref, w_key_ref, w_value_ref, gain_ref, pooled_ref, member_ref, attn_in_ref, keep_ref, send_ref
):
    tiles, _, _ = got_ref.shape
    per_row = LANES // tile
    width = pooled_ref.shape[1]
    blocks = width // LANES
    slots = tiles * tile
    regions = lax.broadcasted_iota(jnp.int32, (REG_DEV, LANES), 0).astype(F32) + 1.0
    hits = jnp.zeros((REG_DEV, LANES), F32)
    for g in range(tiles // per_row):
        row = got_ref[g * per_row, tile * blocks : tile * blocks + 8, :].astype(F32)
        for k in range(1, per_row):
            row = row + got_ref[g * per_row + k, tile * blocks : tile * blocks + 8, :].astype(F32)
        hit = jnp.where(regions == row[0:1, :], 1.0, 0.0)
        hits = hits + hit
        member_ref[:, g * LANES : (g + 1) * LANES] = hit.astype(BF16)
    count = jnp.sum(hits, axis=1, keepdims=True)
    members = member_ref[...]
    sums = [
        mm(members, got_ref[:, c * tile : (c + 1) * tile, :].reshape(slots, LANES))
        for c in range(blocks)
    ]
    pooled = jnp.concatenate(sums, axis=1) * (1.0 / (1.0 + count))
    pooled_ref[...] = pooled
    attn_in = (rms(pooled) * gain_ref[...]).astype(BF16)
    attn_in_ref[...] = attn_in
    low = low_lanes(REG_DEV)
    key = mm(attn_in, w_key_ref[...])
    key = key * lax.rsqrt(mm((key * key).astype(BF16), by_heads()) + EPS)
    value = mm(attn_in, w_value_ref[...])
    zero = jnp.where(low, key, pltpu.roll(value, HEAD_DIM, 1)).astype(BF16)
    one = jnp.where(low, pltpu.roll(key, HEAD_DIM, 1), value).astype(BF16)
    first = group_ref[0] == 0
    keep_ref[...] = jnp.where(first, zero, one)
    send_ref[...] = jnp.where(first, one, zero)


def query_kernel(group_ref, attn_in_ref, w_query_ref, scale_ref, keep_ref, send_ref):
    mine = group_ref[0]
    half = GROUP * HEAD_DIM
    low = low_lanes(REG_DEV)
    for out_ref, group in ((send_ref, 1 - mine), (keep_ref, mine)):
        cols = pl.ds(pl.multiple_of(group * half, half), half)
        query = mm(attn_in_ref[...], w_query_ref[:, cols])
        scale = scale_ref[:, cols]
        for j in range(half // LANES):
            pair = slice(j * LANES, (j + 1) * LANES)
            values = query[:, pair]
            square = mm((values * values).astype(BF16), by_heads())
            unit = values * lax.rsqrt(square + EPS) * scale[:, pair]
            even = jnp.where(low, unit, 0.0).astype(BF16)
            odd = jnp.where(low, pltpu.roll(unit, HEAD_DIM, 1), 0.0).astype(BF16)
            out_ref[:, 2 * j * LANES : (2 * j + 1) * LANES] = even
            out_ref[:, (2 * j + 1) * LANES : (2 * j + 2) * LANES] = odd


def attend_kernel(parts, row_parts, first, last, *refs):
    slabs, kvs = refs[: len(row_parts)], refs[len(row_parts) : len(row_parts) + parts]
    rest = refs[len(row_parts) + parts :]
    key_ref, value_ref, query_ref = rest[-3:]
    acc_in = None if first else rest[0]
    acc_ref = rest[-4]
    out_ref = rest[-5] if last else None
    rows_all = len(row_parts) * REG_DEV
    at = 0
    for kv_ref in kvs:
        kv = kv_ref[...]
        rows = kv.shape[0]
        key_ref[at : at + rows, :] = kv
        value_ref[at : at + rows, :] = jnp.where(low_lanes(rows), jnp.ones_like(kv), kv)
        at += rows
    for r, slab in enumerate(slabs):
        for h in range(GROUP):
            query_ref[h, r * REG_DEV : (r + 1) * REG_DEV, :] = slab[:, h * LANES : (h + 1) * LANES]
    block = max(n for n in range(REG_DEV, 2561, REG_DEV) if at % n == 0)
    span = min(rows_all, 512 if block <= 1024 else 256)

    def step(i, begin):
        keys = pl.ds(pl.multiple_of(i * block, block), block)
        for h in range(GROUP):
            for r in range(rows_all // span):
                here = slice(r * span, (r + 1) * span)
                score = lax.dot_general(
                    query_ref[h, here, :], key_ref[keys, :], NT, preferred_element_type=F32
                )
                new = mm(jnp.exp2(score).astype(BF16), value_ref[keys, :])
                if not begin:
                    new = acc_ref[h, here, :] + new
                elif not first:
                    base = row_parts[0] * REG_DEV if acc_in.shape[1] > rows_all else 0
                    new = acc_in[h, base + r * span : base + (r + 1) * span, :] + new
                acc_ref[h, here, :] = new

    step(0, True)
    if at > block:

        def body(i, carry):
            step(i, False)
            return carry

        lax.fori_loop(1, at // block, body, 0)
    if last:
        low = low_lanes(rows_all)
        for j in range(GROUP // 2):
            a, b = acc_ref[2 * j], acc_ref[2 * j + 1]
            num = jnp.where(low, pltpu.roll(a, HEAD_DIM, 1), b)
            den = jnp.where(low, a, pltpu.roll(b, HEAD_DIM, 1))
            out_ref[:, j * LANES : (j + 1) * LANES] = (num / den).astype(BF16)


def post_kernel(
    group_ref, mine_ref, other_ref, pooled_ref, member_ref, w_out_ref, gain_ref, w_inner_ref, w_outer_ref, out_ref, inner_ref
):
    half = mine_ref.shape[1]
    group = group_ref[0]
    own = pl.ds(pl.multiple_of(group * half, half), half)
    far = pl.ds(pl.multiple_of((1 - group) * half, half), half)
    hidden = (
        pooled_ref[...] + mm(mine_ref[...], w_out_ref[own, :]) + mm(other_ref[...], w_out_ref[far, :])
    )
    mlp_in = (rms(hidden) * gain_ref[...]).astype(BF16)
    inner_width = w_inner_ref.shape[1]
    block = math.gcd(inner_width, 512)
    for j in range(inner_width // block):
        cols = slice(j * block, (j + 1) * block)
        inner_ref[:, cols] = gelu(mm(mlp_in, w_inner_ref[:, cols])).astype(BF16)
    region_out = (hidden + mm(inner_ref[...], w_outer_ref[...])).astype(BF16)
    slots = member_ref.shape[1]
    block = math.gcd(slots, 512)
    for i in range(slots // block):
        rows = slice(i * block, (i + 1) * block)
        out_ref[rows, :] = lax.dot_general(
            member_ref[:, rows], region_out, TN, preferred_element_type=F32
        ).astype(BF16)


def decode_kernel(tile, order, back_ref, sensors_ref, live_ref, gain_ref, w_in_ref, w_out_ref, out_ref):
    step = min(len(order), 32)
    for begin in range(0, len(order), step):
        tiles = [slice(t * tile, (t + 1) * tile) for t in order[begin : begin + step]]
        sensors = jnp.concatenate([sensors_ref[rows, :] for rows in tiles], axis=0)
        back = back_ref[begin * tile : (begin + step) * tile, :]
        total = back.astype(F32) + sensors.astype(F32)
        dec_in = (rms(total) * gain_ref[...]).astype(BF16)
        hidden = gelu(mm(dec_in, w_in_ref[...])).astype(BF16)
        result = mm(hidden, w_out_ref[...])
        for i, rows in enumerate(tiles):
            here = result[i * tile : (i + 1) * tile, :]
            out_ref[rows, :] = jnp.where(live_ref[rows, :] > 0.0, here, 0.0).astype(BF16)


def local(
    order,
    line,
    sensors,
    slot_region,
    w_query,
    w_key,
    w_value,
    w_out,
    temper,
    gain_attn,
    w_inner,
    w_outer,
    gain_mlp,
    gain_dec,
    w_dec_in,
    w_dec_out,
):
    devices = len(order)
    sen_dev, width = sensors.shape
    tile = sen_dev // devices
    me = lax.axis_index(AXIS).astype(jnp.int32).reshape(1)
    core = lax.rem(me, 2)
    place = me // line * line + core * (line // 2) + me % line // 2
    bits = devices.bit_length() - 1
    one, two = 1 << (bits - 2), 1 << (bits - 1)
    group = me // one % 2
    pay_rows = tile * (width // LANES) + 8

    def flipped(value, mask):
        return lax.ppermute(value, AXIS, [(i, i ^ mask) for i in range(devices)])

    def exchanged(value):
        return lax.all_to_all(
            value, AXIS, split_axis=0, concat_axis=0, tiled=True, axis_index_groups=[order]
        )

    payload = pl.pallas_call(
        functools.partial(pack_kernel, tile, order),
        out_shape=jax.ShapeDtypeStruct((devices, pay_rows, LANES), BF16),
        in_specs=[SMEM, VMEM, VMEM],
        out_specs=VMEM,
        compiler_params=PARAMS,
        name="pack",
    )(place, sensors, (slot_region + 1).astype(F32).reshape(-1, LANES))
    got = exchanged(payload)

    scale = jnp.repeat(temper * (math.log2(math.e) / HEAD_DIM), HEAD_DIM).reshape(1, -1)
    live = (slot_region >= 0).astype(F32).reshape(sen_dev, 1)

    kv_shape = jax.ShapeDtypeStruct((REG_DEV, LANES), BF16)
    pooled, members, attn_in, kv_keep, kv_send = pl.pallas_call(
        functools.partial(pool_kernel, tile),
        out_shape=(
            jax.ShapeDtypeStruct((REG_DEV, width), F32),
            jax.ShapeDtypeStruct((REG_DEV, sen_dev), BF16),
            jax.ShapeDtypeStruct((REG_DEV, width), BF16),
            kv_shape,
            kv_shape,
        ),
        in_specs=[SMEM] + [VMEM] * 4,
        out_specs=(VMEM,) * 5,
        compiler_params=PARAMS,
        name="pool",
    )(group, got, w_key, w_value, gain_attn.reshape(1, width))
    kv_other, keep_core = flipped(kv_send, one), flipped(kv_keep, 1)
    keep_core, attn_in = lax.optimization_barrier((keep_core, attn_in))
    slab_shape = jax.ShapeDtypeStruct((REG_DEV, GROUP * LANES), BF16)
    q_keep, q_send = pl.pallas_call(
        query_kernel,
        out_shape=(slab_shape, slab_shape),
        in_specs=[SMEM] + [VMEM] * 3,
        out_specs=(VMEM, VMEM),
        compiler_params=PARAMS,
        cost_estimate=pl.CostEstimate(
            flops=2 * REG_DEV * width * width, bytes_accessed=2 * REG_DEV * width, transcendentals=0
        ),
        name="query",
    )(group, attn_in, w_query, scale)
    slabs = (q_keep, flipped(q_send, one))

    def attend(parts, acc, last=False, row_parts=(0, 1)):
        keys = sum(part.shape[0] for part in parts)
        rows = len(row_parts) * REG_DEV
        acc_shape = (GROUP, rows, LANES)
        work = GROUP * rows * keys
        out_shape = (rows, GROUP * HEAD_DIM) if last else acc_shape
        return pl.pallas_call(
            functools.partial(attend_kernel, len(parts), row_parts, acc is None, last),
            out_shape=jax.ShapeDtypeStruct(out_shape, BF16 if last else F32),
            in_specs=[VMEM] * (len(row_parts) + len(parts) + (acc is not None)),
            out_specs=VMEM,
            scratch_shapes=([pltpu.VMEM(acc_shape, F32)] if last else [])
            + [pltpu.VMEM((keys, LANES), BF16)] * 2
            + [pltpu.VMEM(acc_shape, BF16)],
            compiler_params=PARAMS,
            cost_estimate=pl.CostEstimate(
                flops=work * 4 * 256, bytes_accessed=keys * 2 * LANES, transcendentals=work
            ),
            name="attend",
        )(*(slabs[r] for r in row_parts), *parts, *(() if acc is None else (acc,)))

    own = jnp.concatenate([kv_keep, kv_other], axis=0)
    for bit in range(bits - 3, 2, -1):
        own = jnp.concatenate([own, flipped(own, 1 << bit)], axis=0)
    near, far = 1 << 1, 1 << 2

    hold = lax.optimization_barrier
    a, b = flipped(own, far), flipped(own, near)
    own_two = flipped(own, two)
    own_core = [keep_core, flipped(kv_other, 1)]
    if own.shape[0] > 2 * REG_DEV:
        own_core.append(flipped(own[2 * REG_DEV :], 1))
    acc = attend([own], None)
    own_both = flipped(own_two, 1)
    acc = attend(own_core + [own_two], acc)
    acc, a, b = hold((acc, a, b))

    ab, c = jnp.concatenate([a, b], axis=0), flipped(a, near)
    ab_two, ab_core = flipped(ab, two), flipped(ab, 1)
    acc = attend([ab, own_both], acc)
    acc, c = hold((acc, c))

    c_two, c_core = flipped(c, two), flipped(c, 1)
    acc = attend([c, ab_core], acc)
    acc, ab_two = hold((acc, ab_two))

    ab_both = flipped(ab_two, 1)
    partial = attend([ab_two, c_core], acc, False, (1,))
    partial, ab_both, c_two = hold((partial, ab_both, c_two))

    c_both = flipped(c_two, 1)
    partial = attend([ab_both, c_two], partial, False, (1,))
    theirs = attend([c_both], partial, True, (1,))
    other_heads = flipped(theirs, one)
    mine = attend([ab_two, c_core, ab_both, c_two, c_both], acc, True, (0,))
    mine, other_heads = hold((mine, other_heads))

    back = pl.pallas_call(
        post_kernel,
        out_shape=jax.ShapeDtypeStruct((sen_dev, width), BF16),
        in_specs=[SMEM] + [VMEM] * 8,
        out_specs=VMEM,
        scratch_shapes=[pltpu.VMEM((REG_DEV, w_inner.shape[1]), BF16)],
        compiler_params=PARAMS,
        name="post",
    )(group, mine, other_heads, pooled, members, w_out, gain_mlp.reshape(1, width), w_inner, w_outer)
    returned = exchanged(back.reshape(devices, tile, width)).reshape(sen_dev, width)
    return pl.pallas_call(
        functools.partial(decode_kernel, tile, order),
        out_shape=jax.ShapeDtypeStruct((sen_dev, width), BF16),
        in_specs=[VMEM] * 6,
        out_specs=VMEM,
        compiler_params=PARAMS,
        name="decode",
    )(returned, sensors, live, gain_dec.reshape(1, width), w_dec_in, w_dec_out)


def solution(mesh):
    devices, line = mesh.size, mesh.shape["dp"]
    order = sorted(range(devices), key=lambda i: (i // line, i % 2, i))
    flat = jax.sharding.Mesh(mesh.devices.reshape(-1), (AXIS,))
    placed = (P(AXIS, None), P(AXIS)) + (P(),) * 12
    return jax.shard_map(
        functools.partial(local, order, line),
        mesh=flat,
        in_specs=placed,
        out_specs=P(AXIS, None),
        check_vma=False,
    )
```

```python
import functools
import math

import jax
import jax.numpy as jnp
from jax import lax
from jax.experimental import pallas as pl
from jax.experimental.pallas import tpu as pltpu
from jax.sharding import PartitionSpec as P

HEADS = 8
HEAD_DIM = 64
KV_HEADS = 2
GROUP = HEADS // KV_HEADS
REG_DEV = 256
LANES = 128
EPS = 1e-06
AXIS = "device"
F32 = jnp.float32
BF16 = jnp.bfloat16
NT = (((1,), (1,)), ((), ()))
TN = (((0,), (0,)), ((), ()))

VMEM = pl.BlockSpec(memory_space=pltpu.VMEM)
SMEM = pl.BlockSpec(memory_space=pltpu.SMEM)
PARAMS = pltpu.CompilerParams(vmem_limit_bytes=40 * 1024 * 1024)


def mm(a, b):
    return jnp.dot(a, b, preferred_element_type=F32)


def gelu(values):
    half = 0.5 * values
    slope = math.sqrt(2.0 / math.pi)
    return half + half * jnp.tanh(values * (slope + slope * 0.044715 * values * values))


def rms(values):
    return values * lax.rsqrt(jnp.mean(values * values, axis=-1, keepdims=True) + EPS)


def pack_kernel(tile, order, place_ref, sensors_ref, labels_ref, out_ref):
    per_row = LANES // tile
    blocks = sensors_ref.shape[1] // LANES
    mine = lax.rem(place_ref[0], per_row)
    labels = (labels_ref[...] + 1).astype(F32)
    lane = lax.broadcasted_iota(jnp.int32, labels.shape, 1)
    own_lanes = (lane // tile) == mine
    rolled = []
    for k in range(per_row):
        shift = lax.rem(mine - k + per_row, per_row) * tile
        rolled.append(jnp.where(own_lanes, pltpu.roll(labels, shift, 1), 0.0))
    for at, t in enumerate(order):
        g = t // per_row
        row = jnp.broadcast_to(rolled[t % per_row][g : g + 1, :], (8, LANES)).astype(BF16)
        rows = sensors_ref[t * tile : (t + 1) * tile, :]
        parts = [rows[:, c * LANES : (c + 1) * LANES] for c in range(blocks)]
        out_ref[at] = jnp.concatenate(parts + [row], axis=0)


def by_heads():
    at = lax.broadcasted_iota(jnp.int32, (LANES, LANES), 0) // HEAD_DIM
    to = lax.broadcasted_iota(jnp.int32, (LANES, LANES), 1) // HEAD_DIM
    return jnp.where(at == to, 1.0 / HEAD_DIM, 0.0).astype(BF16)


def low_lanes(rows):
    return lax.broadcasted_iota(jnp.int32, (rows, LANES), 1) < HEAD_DIM


def pool_kernel(
    tile, core_ref, got_ref, w_key_ref, w_value_ref, gain_ref, pooled_ref, member_ref, attn_in_ref, keep_ref, send_ref
):
    tiles, _, _ = got_ref.shape
    per_row = LANES // tile
    width = pooled_ref.shape[1]
    blocks = width // LANES
    slots = tiles * tile
    regions = lax.broadcasted_iota(jnp.int32, (REG_DEV, LANES), 0).astype(F32) + 1.0
    hits = jnp.zeros((REG_DEV, LANES), F32)
    for g in range(tiles // per_row):
        row = got_ref[g * per_row, tile * blocks : tile * blocks + 8, :].astype(F32)
        for k in range(1, per_row):
            row = row + got_ref[g * per_row + k, tile * blocks : tile * blocks + 8, :].astype(F32)
        hit = jnp.where(regions == row[0:1, :], 1.0, 0.0)
        hits = hits + hit
        member_ref[:, g * LANES : (g + 1) * LANES] = hit.astype(BF16)
    count = jnp.sum(hits, axis=1, keepdims=True)
    members = member_ref[...]
    sums = [
        mm(members, got_ref[:, c * tile : (c + 1) * tile, :].reshape(slots, LANES))
        for c in range(blocks)
    ]
    pooled = jnp.concatenate(sums, axis=1) * (1.0 / (1.0 + count))
    pooled_ref[...] = pooled
    attn_in = (rms(pooled) * gain_ref[...]).astype(BF16)
    attn_in_ref[...] = attn_in
    low = low_lanes(REG_DEV)
    key = mm(attn_in, w_key_ref[...])
    key = key * lax.rsqrt(mm((key * key).astype(BF16), by_heads()) + EPS)
    value = mm(attn_in, w_value_ref[...])
    zero = jnp.where(low, key, pltpu.roll(value, HEAD_DIM, 1)).astype(BF16)
    one = jnp.where(low, pltpu.roll(key, HEAD_DIM, 1), value).astype(BF16)
    first = core_ref[0] == 0
    keep_ref[...] = jnp.where(first, zero, one)
    send_ref[...] = jnp.where(first, one, zero)


def query_kernel(core_ref, attn_in_ref, w_query_ref, scale_ref, keep_ref, send_ref):
    core = core_ref[0]
    half = GROUP * HEAD_DIM
    low = low_lanes(REG_DEV)
    for out_ref, group in ((send_ref, 1 - core), (keep_ref, core)):
        cols = pl.ds(pl.multiple_of(group * half, half), half)
        query = mm(attn_in_ref[...], w_query_ref[:, cols])
        scale = scale_ref[:, cols]
        for j in range(half // LANES):
            pair = slice(j * LANES, (j + 1) * LANES)
            values = query[:, pair]
            square = mm((values * values).astype(BF16), by_heads())
            unit = values * lax.rsqrt(square + EPS) * scale[:, pair]
            even = jnp.where(low, unit, 0.0).astype(BF16)
            odd = jnp.where(low, pltpu.roll(unit, HEAD_DIM, 1), 0.0).astype(BF16)
            out_ref[:, 2 * j * LANES : (2 * j + 1) * LANES] = even
            out_ref[:, (2 * j + 1) * LANES : (2 * j + 2) * LANES] = odd


def attend_kernel(parts, row_parts, first, last, *refs):
    slabs, kvs = refs[: len(row_parts)], refs[len(row_parts) : len(row_parts) + parts]
    rest = refs[len(row_parts) + parts :]
    key_ref, value_ref, query_ref = rest[-3:]
    acc_in = None if first else rest[0]
    acc_ref = rest[-4]
    out_ref = rest[-5] if last else None
    rows_all = len(row_parts) * REG_DEV
    at = 0
    for kv_ref in kvs:
        kv = kv_ref[...]
        rows = kv.shape[0]
        key_ref[at : at + rows, :] = kv
        value_ref[at : at + rows, :] = jnp.where(low_lanes(rows), jnp.ones_like(kv), kv)
        at += rows
    for r, slab in enumerate(slabs):
        for h in range(GROUP):
            query_ref[h, r * REG_DEV : (r + 1) * REG_DEV, :] = slab[:, h * LANES : (h + 1) * LANES]
    block = max(n for n in range(REG_DEV, 2561, REG_DEV) if at % n == 0)
    span = min(rows_all, 512 if block <= 1024 else 256)

    def step(i, begin):
        keys = pl.ds(pl.multiple_of(i * block, block), block)
        for h in range(GROUP):
            for r in range(rows_all // span):
                here = slice(r * span, (r + 1) * span)
                score = lax.dot_general(
                    query_ref[h, here, :], key_ref[keys, :], NT, preferred_element_type=F32
                )
                new = mm(jnp.exp2(score).astype(BF16), value_ref[keys, :])
                if not begin:
                    new = acc_ref[h, here, :] + new
                elif not first:
                    base = row_parts[0] * REG_DEV
                    new = acc_in[h, base + r * span : base + (r + 1) * span, :] + new
                acc_ref[h, here, :] = new

    step(0, True)
    if at > block:

        def body(i, carry):
            step(i, False)
            return carry

        lax.fori_loop(1, at // block, body, 0)
    if last:
        low = low_lanes(rows_all)
        for j in range(GROUP // 2):
            a, b = acc_ref[2 * j], acc_ref[2 * j + 1]
            num = jnp.where(low, pltpu.roll(a, HEAD_DIM, 1), b)
            den = jnp.where(low, a, pltpu.roll(b, HEAD_DIM, 1))
            out_ref[:, j * LANES : (j + 1) * LANES] = (num / den).astype(BF16)


def post_kernel(
    core_ref, mine_ref, other_ref, pooled_ref, member_ref, w_out_ref, gain_ref, w_inner_ref, w_outer_ref, out_ref, inner_ref
):
    half = mine_ref.shape[1]
    core = core_ref[0]
    own = pl.ds(pl.multiple_of(core * half, half), half)
    far = pl.ds(pl.multiple_of((1 - core) * half, half), half)
    hidden = (
        pooled_ref[...] + mm(mine_ref[...], w_out_ref[own, :]) + mm(other_ref[...], w_out_ref[far, :])
    )
    mlp_in = (rms(hidden) * gain_ref[...]).astype(BF16)
    inner_width = w_inner_ref.shape[1]
    block = math.gcd(inner_width, 512)
    for j in range(inner_width // block):
        cols = slice(j * block, (j + 1) * block)
        inner_ref[:, cols] = gelu(mm(mlp_in, w_inner_ref[:, cols])).astype(BF16)
    region_out = (hidden + mm(inner_ref[...], w_outer_ref[...])).astype(BF16)
    slots = member_ref.shape[1]
    block = math.gcd(slots, 512)
    for i in range(slots // block):
        rows = slice(i * block, (i + 1) * block)
        out_ref[rows, :] = lax.dot_general(
            member_ref[:, rows], region_out, TN, preferred_element_type=F32
        ).astype(BF16)


def decode_kernel(tile, order, back_ref, sensors_ref, live_ref, gain_ref, w_in_ref, w_out_ref, out_ref):
    step = min(len(order), 32)
    for begin in range(0, len(order), step):
        tiles = [slice(t * tile, (t + 1) * tile) for t in order[begin : begin + step]]
        sensors = jnp.concatenate([sensors_ref[rows, :] for rows in tiles], axis=0)
        back = back_ref[begin * tile : (begin + step) * tile, :]
        total = back.astype(F32) + sensors.astype(F32)
        dec_in = (rms(total) * gain_ref[...]).astype(BF16)
        hidden = gelu(mm(dec_in, w_in_ref[...])).astype(BF16)
        result = mm(hidden, w_out_ref[...])
        for i, rows in enumerate(tiles):
            here = result[i * tile : (i + 1) * tile, :]
            out_ref[rows, :] = jnp.where(live_ref[rows, :] > 0.0, here, 0.0).astype(BF16)


def local(
    order,
    line,
    sensors,
    slot_region,
    w_query,
    w_key,
    w_value,
    w_out,
    temper,
    gain_attn,
    w_inner,
    w_outer,
    gain_mlp,
    gain_dec,
    w_dec_in,
    w_dec_out,
):
    devices = len(order)
    sen_dev, width = sensors.shape
    tile = sen_dev // devices
    me = lax.axis_index(AXIS).astype(jnp.int32).reshape(1)
    core = lax.rem(me, 2)
    place = me // line * line + core * (line // 2) + me % line // 2
    bits = devices.bit_length() - 1
    pay_rows = tile * (width // LANES) + 8

    def flipped(value, mask):
        return lax.ppermute(value, AXIS, [(i, i ^ mask) for i in range(devices)])

    def exchanged(value):
        return lax.all_to_all(
            value, AXIS, split_axis=0, concat_axis=0, tiled=True, axis_index_groups=[order]
        )

    payload = pl.pallas_call(
        functools.partial(pack_kernel, tile, order),
        out_shape=jax.ShapeDtypeStruct((devices, pay_rows, LANES), BF16),
        in_specs=[SMEM, VMEM, VMEM],
        out_specs=VMEM,
        compiler_params=PARAMS,
        name="pack",
    )(place, sensors, slot_region.reshape(-1, LANES))
    got = exchanged(payload)

    scale = jnp.repeat(temper * (math.log2(math.e) / HEAD_DIM), HEAD_DIM).reshape(1, -1)
    live = (slot_region >= 0).astype(F32).reshape(sen_dev, 1)

    kv_shape = jax.ShapeDtypeStruct((REG_DEV, LANES), BF16)
    pooled, members, attn_in, kv_keep, kv_send = pl.pallas_call(
        functools.partial(pool_kernel, tile),
        out_shape=(
            jax.ShapeDtypeStruct((REG_DEV, width), F32),
            jax.ShapeDtypeStruct((REG_DEV, sen_dev), BF16),
            jax.ShapeDtypeStruct((REG_DEV, width), BF16),
            kv_shape,
            kv_shape,
        ),
        in_specs=[SMEM] + [VMEM] * 4,
        out_specs=(VMEM,) * 5,
        compiler_params=PARAMS,
        name="pool",
    )(core, got, w_key, w_value, gain_attn.reshape(1, width))
    kv_other = flipped(kv_send, 1)
    slab_shape = jax.ShapeDtypeStruct((REG_DEV, GROUP * LANES), BF16)
    q_keep, q_send = pl.pallas_call(
        query_kernel,
        out_shape=(slab_shape, slab_shape),
        in_specs=[SMEM] + [VMEM] * 3,
        out_specs=(VMEM, VMEM),
        compiler_params=PARAMS,
        cost_estimate=pl.CostEstimate(
            flops=2 * REG_DEV * width * width, bytes_accessed=2 * REG_DEV * width, transcendentals=0
        ),
        name="query",
    )(core, attn_in, w_query, scale)
    kv_other, q_keep, q_send = lax.optimization_barrier((kv_other, q_keep, q_send))
    slabs = (q_keep, flipped(q_send, 1))

    def attend(parts, acc, last=False, row_parts=(0, 1)):
        keys = sum(part.shape[0] for part in parts)
        rows = len(row_parts) * REG_DEV
        acc_shape = (GROUP, rows, LANES)
        work = GROUP * rows * keys
        out_shape = (rows, GROUP * HEAD_DIM) if last else acc_shape
        return pl.pallas_call(
            functools.partial(attend_kernel, len(parts), row_parts, acc is None, last),
            out_shape=jax.ShapeDtypeStruct(out_shape, BF16 if last else F32),
            in_specs=[VMEM] * (len(row_parts) + len(parts) + (acc is not None)),
            out_specs=VMEM,
            scratch_shapes=([pltpu.VMEM(acc_shape, F32)] if last else [])
            + [pltpu.VMEM((keys, LANES), BF16)] * 2
            + [pltpu.VMEM(acc_shape, BF16)],
            compiler_params=PARAMS,
            cost_estimate=pl.CostEstimate(
                flops=work, bytes_accessed=keys * 2 * LANES, transcendentals=0
            ),
            name="attend",
        )(*(slabs[r] for r in row_parts), *parts, *(() if acc is None else (acc,)))

    one, two = 1 << (bits - 2), 1 << (bits - 1)
    own = jnp.concatenate([kv_keep, kv_other], axis=0)
    for bit in range(bits - 3, 2, -1):
        own = jnp.concatenate([own, flipped(own, 1 << bit)], axis=0)
    near, far = 1 << 1, 1 << 2

    hold = lax.optimization_barrier
    a, b = flipped(own, far), flipped(own, near)
    own_one, own_two = flipped(own, one), flipped(own, two)
    acc = attend([own], None)
    acc, a, b, own_one, own_two = hold((acc, a, b, own_one, own_two))
    ab, c = jnp.concatenate([a, b], axis=0), flipped(a, near)
    ab_one, ab_two, own_corner = flipped(ab, one), flipped(ab, two), flipped(own_two, one)
    acc = attend([ab, own_one, own_two], acc)
    acc, c, ab_one, ab_two = hold((acc, c, ab_one, ab_two))
    c_one, c_two, ab_corner = flipped(c, one), flipped(c, two), flipped(ab_one, two)
    acc = attend([c, ab_one, ab_two, own_corner], acc)
    acc, c_one, c_two = hold((acc, c_one, c_two))
    c_corner = flipped(c_two, one)
    acc = attend([c_one, c_two, ab_corner], acc)

    theirs = attend([c_corner], acc, True, (1,))
    other_heads = flipped(theirs, 1)
    mine = attend([c_corner], acc, True, (0,))
    mine, other_heads = lax.optimization_barrier((mine, other_heads))

    back = pl.pallas_call(
        post_kernel,
        out_shape=jax.ShapeDtypeStruct((sen_dev, width), BF16),
        in_specs=[SMEM] + [VMEM] * 8,
        out_specs=VMEM,
        scratch_shapes=[pltpu.VMEM((REG_DEV, w_inner.shape[1]), BF16)],
        compiler_params=PARAMS,
        name="post",
    )(core, mine, other_heads, pooled, members, w_out, gain_mlp.reshape(1, width), w_inner, w_outer)
    returned = exchanged(back.reshape(devices, tile, width)).reshape(sen_dev, width)
    return pl.pallas_call(
        functools.partial(decode_kernel, tile, order),
        out_shape=jax.ShapeDtypeStruct((sen_dev, width), BF16),
        in_specs=[VMEM] * 6,
        out_specs=VMEM,
        compiler_params=PARAMS,
        name="decode",
    )(returned, sensors, live, gain_dec.reshape(1, width), w_dec_in, w_dec_out)


def solution(mesh):
    devices, line = mesh.size, mesh.shape["dp"]
    order = sorted(range(devices), key=lambda i: (i // line, i % 2, i))
    flat = jax.sharding.Mesh(mesh.devices.reshape(-1), (AXIS,))
    placed = (P(AXIS, None), P(AXIS)) + (P(),) * 12
    return jax.shard_map(
        functools.partial(local, order, line),
        mesh=flat,
        in_specs=placed,
        out_specs=P(AXIS, None),
        check_vma=False,
    )
```

```python
import functools
import math

import jax
import jax.numpy as jnp
from jax import lax
from jax.experimental import pallas as pl
from jax.experimental.pallas import tpu as pltpu
from jax.sharding import PartitionSpec as P

HEADS = 8
HEAD_DIM = 64
KV_HEADS = 2
GROUP = HEADS // KV_HEADS
REG_DEV = 256
LANES = 128
EPS = 1e-06
AXIS = "device"
ORDER = (
    30, 6, 18, 15, 11, 23, 7, 13, 3, 14, 28, 12, 26, 5, 24, 21,
    8, 0, 27, 16, 1, 4, 22, 17, 19, 9, 25, 29, 10, 31, 20, 2,
)
F32 = jnp.float32
BF16 = jnp.bfloat16
NT = (((1,), (1,)), ((), ()))
TN = (((0,), (0,)), ((), ()))

VMEM = pl.BlockSpec(memory_space=pltpu.VMEM)
SMEM = pl.BlockSpec(memory_space=pltpu.SMEM)
PARAMS = pltpu.CompilerParams(vmem_limit_bytes=40 * 1024 * 1024)


def mm(a, b):
    return jnp.dot(a, b, preferred_element_type=F32)


def gelu(values):
    half = 0.5 * values
    slope = math.sqrt(2.0 / math.pi)
    return half + half * jnp.tanh(values * (slope + slope * 0.044715 * values * values))


def rms(values):
    return values * lax.rsqrt(jnp.mean(values * values, axis=-1, keepdims=True) + EPS)


def pack_kernel(tile, order, me_ref, core_ref, sensors_ref, labels_ref, out_ref):
    per_row = LANES // tile
    blocks = sensors_ref.shape[1] // LANES
    me, mine = me_ref[0], jnp.int32(0)
    for at, i in enumerate(order):
        mine = jnp.where(me == i, at % per_row, mine)
    labels = (labels_ref[...] + 1).astype(F32)
    lane = lax.broadcasted_iota(jnp.int32, labels.shape, 1)
    own_lanes = (lane // tile) == mine
    rolled = []
    for k in range(per_row):
        shift = lax.rem(mine - k + per_row, per_row) * tile
        rolled.append(jnp.where(own_lanes, pltpu.roll(labels, shift, 1), 0.0))
    for at, t in enumerate(order):
        g = t // per_row
        row = jnp.broadcast_to(rolled[t % per_row][g : g + 1, :], (8, LANES)).astype(BF16)
        rows = sensors_ref[t * tile : (t + 1) * tile, :]
        parts = [rows[:, c * LANES : (c + 1) * LANES] for c in range(blocks)]
        out_ref[at] = jnp.concatenate(parts + [row], axis=0)


def by_heads():
    at = lax.broadcasted_iota(jnp.int32, (LANES, LANES), 0) // HEAD_DIM
    to = lax.broadcasted_iota(jnp.int32, (LANES, LANES), 1) // HEAD_DIM
    return jnp.where(at == to, 1.0 / HEAD_DIM, 0.0).astype(BF16)


def low_lanes(rows):
    return lax.broadcasted_iota(jnp.int32, (rows, LANES), 1) < HEAD_DIM


def pool_kernel(
    tile, core_ref, got_ref, w_key_ref, w_value_ref, gain_ref, pooled_ref, member_ref, attn_in_ref, keep_ref, send_ref
):
    tiles, _, _ = got_ref.shape
    per_row = LANES // tile
    width = pooled_ref.shape[1]
    blocks = width // LANES
    slots = tiles * tile
    regions = lax.broadcasted_iota(jnp.int32, (REG_DEV, LANES), 0).astype(F32) + 1.0
    hits = jnp.zeros((REG_DEV, LANES), F32)
    for g in range(tiles // per_row):
        row = got_ref[g * per_row, tile * blocks : tile * blocks + 8, :].astype(F32)
        for k in range(1, per_row):
            row = row + got_ref[g * per_row + k, tile * blocks : tile * blocks + 8, :].astype(F32)
        hit = jnp.where(regions == row[0:1, :], 1.0, 0.0)
        hits = hits + hit
        member_ref[:, g * LANES : (g + 1) * LANES] = hit.astype(BF16)
    count = jnp.sum(hits, axis=1, keepdims=True)
    members = member_ref[...]
    sums = [
        mm(members, got_ref[:, c * tile : (c + 1) * tile, :].reshape(slots, LANES))
        for c in range(blocks)
    ]
    pooled = jnp.concatenate(sums, axis=1) * (1.0 / (1.0 + count))
    pooled_ref[...] = pooled
    attn_in = (rms(pooled) * gain_ref[...]).astype(BF16)
    attn_in_ref[...] = attn_in
    low = low_lanes(REG_DEV)
    key = mm(attn_in, w_key_ref[...])
    key = key * lax.rsqrt(mm((key * key).astype(BF16), by_heads()) + EPS)
    value = mm(attn_in, w_value_ref[...])
    zero = jnp.where(low, key, pltpu.roll(value, HEAD_DIM, 1)).astype(BF16)
    one = jnp.where(low, pltpu.roll(key, HEAD_DIM, 1), value).astype(BF16)
    first = core_ref[0] == 0
    keep_ref[...] = jnp.where(first, zero, one)
    send_ref[...] = jnp.where(first, one, zero)


def query_kernel(core_ref, attn_in_ref, w_query_ref, scale_ref, keep_ref, send_ref):
    core = core_ref[0]
    half = GROUP * HEAD_DIM
    low = low_lanes(REG_DEV)
    for out_ref, group in ((send_ref, 1 - core), (keep_ref, core)):
        cols = pl.ds(pl.multiple_of(group * half, half), half)
        query = mm(attn_in_ref[...], w_query_ref[:, cols])
        scale = scale_ref[:, cols]
        for j in range(half // LANES):
            pair = slice(j * LANES, (j + 1) * LANES)
            values = query[:, pair]
            square = mm((values * values).astype(BF16), by_heads())
            unit = values * lax.rsqrt(square + EPS) * scale[:, pair]
            even = jnp.where(low, unit, 0.0).astype(BF16)
            odd = jnp.where(low, pltpu.roll(unit, HEAD_DIM, 1), 0.0).astype(BF16)
            out_ref[:, 2 * j * LANES : (2 * j + 1) * LANES] = even
            out_ref[:, (2 * j + 1) * LANES : (2 * j + 2) * LANES] = odd


def attend_kernel(parts, row_parts, first, last, *refs):
    slabs, kvs = refs[: len(row_parts)], refs[len(row_parts) : len(row_parts) + parts]
    rest = refs[len(row_parts) + parts :]
    key_ref, value_ref, query_ref = rest[-3:]
    acc_in = None if first else rest[0]
    acc_ref = rest[-4]
    out_ref = rest[-5] if last else None
    rows_all = len(row_parts) * REG_DEV
    at = 0
    for kv_ref in kvs:
        kv = kv_ref[...]
        rows = kv.shape[0]
        key_ref[at : at + rows, :] = kv
        value_ref[at : at + rows, :] = jnp.where(low_lanes(rows), jnp.ones_like(kv), kv)
        at += rows
    for r, slab in enumerate(slabs):
        for h in range(GROUP):
            query_ref[h, r * REG_DEV : (r + 1) * REG_DEV, :] = slab[:, h * LANES : (h + 1) * LANES]
    block = max(n for n in range(REG_DEV, 2561, REG_DEV) if at % n == 0)
    span = min(rows_all, 512 if block <= 1024 else 256)

    def step(i, begin):
        keys = pl.ds(pl.multiple_of(i * block, block), block)
        for h in range(GROUP):
            for r in range(rows_all // span):
                here = slice(r * span, (r + 1) * span)
                score = lax.dot_general(
                    query_ref[h, here, :], key_ref[keys, :], NT, preferred_element_type=F32
                )
                new = mm(jnp.exp2(score).astype(BF16), value_ref[keys, :])
                if not begin:
                    new = acc_ref[h, here, :] + new
                elif not first:
                    base = row_parts[0] * REG_DEV
                    new = acc_in[h, base + r * span : base + (r + 1) * span, :] + new
                acc_ref[h, here, :] = new

    step(0, True)
    if at > block:

        def body(i, carry):
            step(i, False)
            return carry

        lax.fori_loop(1, at // block, body, 0)
    if last:
        low = low_lanes(rows_all)
        for j in range(GROUP // 2):
            a, b = acc_ref[2 * j], acc_ref[2 * j + 1]
            num = jnp.where(low, pltpu.roll(a, HEAD_DIM, 1), b)
            den = jnp.where(low, a, pltpu.roll(b, HEAD_DIM, 1))
            out_ref[:, j * LANES : (j + 1) * LANES] = (num / den).astype(BF16)


def post_kernel(
    core_ref, mine_ref, other_ref, pooled_ref, member_ref, w_out_ref, gain_ref, w_inner_ref, w_outer_ref, out_ref, inner_ref
):
    half = mine_ref.shape[1]
    core = core_ref[0]
    own = pl.ds(pl.multiple_of(core * half, half), half)
    far = pl.ds(pl.multiple_of((1 - core) * half, half), half)
    hidden = (
        pooled_ref[...] + mm(mine_ref[...], w_out_ref[own, :]) + mm(other_ref[...], w_out_ref[far, :])
    )
    mlp_in = (rms(hidden) * gain_ref[...]).astype(BF16)
    inner_width = w_inner_ref.shape[1]
    block = math.gcd(inner_width, 512)
    for j in range(inner_width // block):
        cols = slice(j * block, (j + 1) * block)
        inner_ref[:, cols] = gelu(mm(mlp_in, w_inner_ref[:, cols])).astype(BF16)
    region_out = (hidden + mm(inner_ref[...], w_outer_ref[...])).astype(BF16)
    slots = member_ref.shape[1]
    block = math.gcd(slots, 512)
    for i in range(slots // block):
        rows = slice(i * block, (i + 1) * block)
        out_ref[rows, :] = lax.dot_general(
            member_ref[:, rows], region_out, TN, preferred_element_type=F32
        ).astype(BF16)


def decode_kernel(tile, order, back_ref, sensors_ref, live_ref, gain_ref, w_in_ref, w_out_ref, out_ref):
    step = min(len(order), 32)
    for begin in range(0, len(order), step):
        tiles = [slice(t * tile, (t + 1) * tile) for t in order[begin : begin + step]]
        sensors = jnp.concatenate([sensors_ref[rows, :] for rows in tiles], axis=0)
        back = back_ref[begin * tile : (begin + step) * tile, :]
        total = back.astype(F32) + sensors.astype(F32)
        dec_in = (rms(total) * gain_ref[...]).astype(BF16)
        hidden = gelu(mm(dec_in, w_in_ref[...])).astype(BF16)
        result = mm(hidden, w_out_ref[...])
        for i, rows in enumerate(tiles):
            here = result[i * tile : (i + 1) * tile, :]
            out_ref[rows, :] = jnp.where(live_ref[rows, :] > 0.0, here, 0.0).astype(BF16)


def local(
    order,
    sensors,
    slot_region,
    w_query,
    w_key,
    w_value,
    w_out,
    temper,
    gain_attn,
    w_inner,
    w_outer,
    gain_mlp,
    gain_dec,
    w_dec_in,
    w_dec_out,
):
    devices = len(order)
    sen_dev, width = sensors.shape
    tile = sen_dev // devices
    me = lax.axis_index(AXIS).astype(jnp.int32).reshape(1)
    core = lax.rem(me, 2)
    bits = devices.bit_length() - 1
    pay_rows = tile * (width // LANES) + 8

    def flipped(value, mask):
        return lax.ppermute(value, AXIS, [(i, i ^ mask) for i in range(devices)])

    def exchanged(value):
        return lax.all_to_all(
            value, AXIS, split_axis=0, concat_axis=0, tiled=True, axis_index_groups=[order]
        )

    payload = pl.pallas_call(
        functools.partial(pack_kernel, tile, order),
        out_shape=jax.ShapeDtypeStruct((devices, pay_rows, LANES), BF16),
        in_specs=[SMEM, SMEM, VMEM, VMEM],
        out_specs=VMEM,
        compiler_params=PARAMS,
        name="pack",
    )(me, core, sensors, slot_region.reshape(-1, LANES))
    got = exchanged(payload)

    scale = jnp.repeat(temper * (math.log2(math.e) / HEAD_DIM), HEAD_DIM).reshape(1, -1)
    live = (slot_region >= 0).astype(F32).reshape(sen_dev, 1)

    kv_shape = jax.ShapeDtypeStruct((REG_DEV, LANES), BF16)
    pooled, members, attn_in, kv_keep, kv_send = pl.pallas_call(
        functools.partial(pool_kernel, tile),
        out_shape=(
            jax.ShapeDtypeStruct((REG_DEV, width), F32),
            jax.ShapeDtypeStruct((REG_DEV, sen_dev), BF16),
            jax.ShapeDtypeStruct((REG_DEV, width), BF16),
            kv_shape,
            kv_shape,
        ),
        in_specs=[SMEM] + [VMEM] * 4,
        out_specs=(VMEM,) * 5,
        compiler_params=PARAMS,
        name="pool",
    )(core, got, w_key, w_value, gain_attn.reshape(1, width))
    kv_other = flipped(kv_send, 1)
    slab_shape = jax.ShapeDtypeStruct((REG_DEV, GROUP * LANES), BF16)
    q_keep, q_send = pl.pallas_call(
        query_kernel,
        out_shape=(slab_shape, slab_shape),
        in_specs=[SMEM] + [VMEM] * 3,
        out_specs=(VMEM, VMEM),
        compiler_params=PARAMS,
        cost_estimate=pl.CostEstimate(
            flops=2 * REG_DEV * width * width, bytes_accessed=2 * REG_DEV * width, transcendentals=0
        ),
        name="query",
    )(core, attn_in, w_query, scale)
    kv_other, q_keep, q_send = lax.optimization_barrier((kv_other, q_keep, q_send))
    slabs = (q_keep, flipped(q_send, 1))

    def attend(parts, acc, last=False, row_parts=(0, 1)):
        keys = sum(part.shape[0] for part in parts)
        rows = len(row_parts) * REG_DEV
        acc_shape = (GROUP, rows, LANES)
        work = GROUP * rows * keys
        out_shape = (rows, GROUP * HEAD_DIM) if last else acc_shape
        return pl.pallas_call(
            functools.partial(attend_kernel, len(parts), row_parts, acc is None, last),
            out_shape=jax.ShapeDtypeStruct(out_shape, BF16 if last else F32),
            in_specs=[VMEM] * (len(row_parts) + len(parts) + (acc is not None)),
            out_specs=VMEM,
            scratch_shapes=([pltpu.VMEM(acc_shape, F32)] if last else [])
            + [pltpu.VMEM((keys, LANES), BF16)] * 2
            + [pltpu.VMEM(acc_shape, BF16)],
            compiler_params=PARAMS,
            cost_estimate=pl.CostEstimate(
                flops=work, bytes_accessed=keys * 2 * LANES, transcendentals=0
            ),
            name="attend",
        )(*(slabs[r] for r in row_parts), *parts, *(() if acc is None else (acc,)))

    one, two = 1 << (bits - 2), 1 << (bits - 1)
    own = jnp.concatenate([kv_keep, kv_other], axis=0)
    for bit in range(bits - 3, 2, -1):
        own = jnp.concatenate([own, flipped(own, 1 << bit)], axis=0)
    near, far = 1 << 1, 1 << 2

    hold = lax.optimization_barrier
    a, b = flipped(own, far), flipped(own, near)
    own_one, own_two = flipped(own, one), flipped(own, two)
    acc = attend([own], None)
    acc, a, b, own_one, own_two = hold((acc, a, b, own_one, own_two))
    ab, c = jnp.concatenate([a, b], axis=0), flipped(a, near)
    ab_one, ab_two, own_corner = flipped(ab, one), flipped(ab, two), flipped(own_two, one)
    acc = attend([ab, own_one, own_two], acc)
    acc, c, ab_one, ab_two = hold((acc, c, ab_one, ab_two))
    c_one, c_two, ab_corner = flipped(c, one), flipped(c, two), flipped(ab_one, two)
    acc = attend([c, ab_one, ab_two, own_corner], acc)
    acc, c_one, c_two = hold((acc, c_one, c_two))
    c_corner = flipped(c_two, one)
    acc = attend([c_one, c_two, ab_corner], acc)

    theirs = attend([c_corner], acc, True, (1,))
    other_heads = flipped(theirs, 1)
    mine = attend([c_corner], acc, True, (0,))
    mine, other_heads = lax.optimization_barrier((mine, other_heads))

    back = pl.pallas_call(
        post_kernel,
        out_shape=jax.ShapeDtypeStruct((sen_dev, width), BF16),
        in_specs=[SMEM] + [VMEM] * 8,
        out_specs=VMEM,
        scratch_shapes=[pltpu.VMEM((REG_DEV, w_inner.shape[1]), BF16)],
        compiler_params=PARAMS,
        name="post",
    )(core, mine, other_heads, pooled, members, w_out, gain_mlp.reshape(1, width), w_inner, w_outer)
    returned = exchanged(back.reshape(devices, tile, width)).reshape(sen_dev, width)
    return pl.pallas_call(
        functools.partial(decode_kernel, tile, order),
        out_shape=jax.ShapeDtypeStruct((sen_dev, width), BF16),
        in_specs=[VMEM] * 6,
        out_specs=VMEM,
        compiler_params=PARAMS,
        name="decode",
    )(returned, sensors, live, gain_dec.reshape(1, width), w_dec_in, w_dec_out)


def solution(mesh):
    devices, line = mesh.size, mesh.shape["dp"]
    order = sorted(range(devices), key=lambda i: (i // line, i % 2, i))
    if devices == len(ORDER):
        order = list(ORDER)
    flat = jax.sharding.Mesh(mesh.devices.reshape(-1), (AXIS,))
    placed = (P(AXIS, None), P(AXIS)) + (P(),) * 12
    return jax.shard_map(
        functools.partial(local, order),
        mesh=flat,
        in_specs=placed,
        out_specs=P(AXIS, None),
        check_vma=False,
    )
```

```python
import functools
import math

import jax
import jax.numpy as jnp
from jax import lax
from jax.experimental import pallas as pl
from jax.experimental.pallas import tpu as pltpu
from jax.sharding import PartitionSpec as P

HEADS = 8
HEAD_DIM = 64
KV_HEADS = 2
GROUP = HEADS // KV_HEADS
REG_DEV = 256
LANES = 128
EPS = 1e-06
AXIS = "device"
ORDER = (
    30, 6, 18, 15, 11, 23, 7, 13, 3, 14, 28, 12, 26, 5, 24, 21,
    8, 0, 27, 16, 1, 4, 22, 17, 19, 9, 25, 29, 10, 31, 20, 2,
)
F32 = jnp.float32
BF16 = jnp.bfloat16
NT = (((1,), (1,)), ((), ()))
TN = (((0,), (0,)), ((), ()))

VMEM = pl.BlockSpec(memory_space=pltpu.VMEM)
SMEM = pl.BlockSpec(memory_space=pltpu.SMEM)
PARAMS = pltpu.CompilerParams(vmem_limit_bytes=40 * 1024 * 1024)


def mm(a, b):
    return jnp.dot(a, b, preferred_element_type=F32)


def gelu(values):
    half = 0.5 * values
    slope = math.sqrt(2.0 / math.pi)
    return half + half * jnp.tanh(values * (slope + slope * 0.044715 * values * values))


def rms(values):
    return values * lax.rsqrt(jnp.mean(values * values, axis=-1, keepdims=True) + EPS)


def pack_kernel(tile, order, me_ref, core_ref, sensors_ref, labels_ref, out_ref):
    per_row = LANES // tile
    blocks = sensors_ref.shape[1] // LANES
    me, mine = me_ref[0], jnp.int32(0)
    for at, i in enumerate(order):
        mine = jnp.where(me == i, at % per_row, mine)
    labels = (labels_ref[...] + 1).astype(F32)
    lane = lax.broadcasted_iota(jnp.int32, labels.shape, 1)
    own_lanes = (lane // tile) == mine
    rolled = []
    for k in range(per_row):
        shift = lax.rem(mine - k + per_row, per_row) * tile
        rolled.append(jnp.where(own_lanes, pltpu.roll(labels, shift, 1), 0.0))
    for at, t in enumerate(order):
        g = t // per_row
        row = jnp.broadcast_to(rolled[t % per_row][g : g + 1, :], (8, LANES)).astype(BF16)
        rows = sensors_ref[t * tile : (t + 1) * tile, :]
        parts = [rows[:, c * LANES : (c + 1) * LANES] for c in range(blocks)]
        out_ref[at] = jnp.concatenate(parts + [row], axis=0)


def by_heads():
    at = lax.broadcasted_iota(jnp.int32, (LANES, LANES), 0) // HEAD_DIM
    to = lax.broadcasted_iota(jnp.int32, (LANES, LANES), 1) // HEAD_DIM
    return jnp.where(at == to, 1.0 / HEAD_DIM, 0.0).astype(BF16)


def low_lanes(rows):
    return lax.broadcasted_iota(jnp.int32, (rows, LANES), 1) < HEAD_DIM


def pool_kernel(
    tile, core_ref, got_ref, w_key_ref, w_value_ref, gain_ref, pooled_ref, member_ref, attn_in_ref, keep_ref, send_ref
):
    tiles, _, _ = got_ref.shape
    per_row = LANES // tile
    width = pooled_ref.shape[1]
    blocks = width // LANES
    slots = tiles * tile
    regions = lax.broadcasted_iota(jnp.int32, (REG_DEV, LANES), 0).astype(F32) + 1.0
    hits = jnp.zeros((REG_DEV, LANES), F32)
    for g in range(tiles // per_row):
        row = got_ref[g * per_row, tile * blocks : tile * blocks + 8, :].astype(F32)
        for k in range(1, per_row):
            row = row + got_ref[g * per_row + k, tile * blocks : tile * blocks + 8, :].astype(F32)
        hit = jnp.where(regions == row[0:1, :], 1.0, 0.0)
        hits = hits + hit
        member_ref[:, g * LANES : (g + 1) * LANES] = hit.astype(BF16)
    count = jnp.sum(hits, axis=1, keepdims=True)
    members = member_ref[...]
    sums = [
        mm(members, got_ref[:, c * tile : (c + 1) * tile, :].reshape(slots, LANES))
        for c in range(blocks)
    ]
    pooled = jnp.concatenate(sums, axis=1) * (1.0 / (1.0 + count))
    pooled_ref[...] = pooled
    attn_in = (rms(pooled) * gain_ref[...]).astype(BF16)
    attn_in_ref[...] = attn_in
    low = low_lanes(REG_DEV)
    key = mm(attn_in, w_key_ref[...])
    key = key * lax.rsqrt(mm((key * key).astype(BF16), by_heads()) + EPS)
    value = mm(attn_in, w_value_ref[...])
    zero = jnp.where(low, key, pltpu.roll(value, HEAD_DIM, 1)).astype(BF16)
    one = jnp.where(low, pltpu.roll(key, HEAD_DIM, 1), value).astype(BF16)
    first = core_ref[0] == 0
    keep_ref[...] = jnp.where(first, zero, one)
    send_ref[...] = jnp.where(first, one, zero)


def query_kernel(core_ref, attn_in_ref, w_query_ref, scale_ref, keep_ref, send_ref):
    core = core_ref[0]
    half = GROUP * HEAD_DIM
    low = low_lanes(REG_DEV)
    for out_ref, group in ((send_ref, 1 - core), (keep_ref, core)):
        cols = pl.ds(pl.multiple_of(group * half, half), half)
        query = mm(attn_in_ref[...], w_query_ref[:, cols])
        scale = scale_ref[:, cols]
        for j in range(half // LANES):
            pair = slice(j * LANES, (j + 1) * LANES)
            values = query[:, pair]
            square = mm((values * values).astype(BF16), by_heads())
            unit = values * lax.rsqrt(square + EPS) * scale[:, pair]
            even = jnp.where(low, unit, 0.0).astype(BF16)
            odd = jnp.where(low, pltpu.roll(unit, HEAD_DIM, 1), 0.0).astype(BF16)
            out_ref[:, 2 * j * LANES : (2 * j + 1) * LANES] = even
            out_ref[:, (2 * j + 1) * LANES : (2 * j + 2) * LANES] = odd


def attend_kernel(parts, row_parts, first, last, *refs):
    slabs, kvs = refs[: len(row_parts)], refs[len(row_parts) : len(row_parts) + parts]
    rest = refs[len(row_parts) + parts :]
    key_ref, value_ref, query_ref = rest[-3:]
    acc_in = None if first else rest[0]
    acc_ref = rest[-4]
    out_ref = rest[-5] if last else None
    rows_all = len(row_parts) * REG_DEV
    at = 0
    for kv_ref in kvs:
        kv = kv_ref[...]
        rows = kv.shape[0]
        key_ref[at : at + rows, :] = kv
        value_ref[at : at + rows, :] = jnp.where(low_lanes(rows), jnp.ones_like(kv), kv)
        at += rows
    for r, slab in enumerate(slabs):
        for h in range(GROUP):
            query_ref[h, r * REG_DEV : (r + 1) * REG_DEV, :] = slab[:, h * LANES : (h + 1) * LANES]
    block = max(n for n in range(REG_DEV, 3073, REG_DEV) if at % n == 0)
    span = min(rows_all, 512 if block <= 1024 else 256)

    def step(i, begin):
        keys = pl.ds(pl.multiple_of(i * block, block), block)
        for h in range(GROUP):
            for r in range(rows_all // span):
                here = slice(r * span, (r + 1) * span)
                score = lax.dot_general(
                    query_ref[h, here, :], key_ref[keys, :], NT, preferred_element_type=F32
                )
                new = mm(jnp.exp2(score).astype(BF16), value_ref[keys, :])
                if not begin:
                    new = acc_ref[h, here, :] + new
                elif not first:
                    base = row_parts[0] * REG_DEV
                    new = acc_in[h, base + r * span : base + (r + 1) * span, :] + new
                acc_ref[h, here, :] = new

    step(0, True)
    if at > block:

        def body(i, carry):
            step(i, False)
            return carry

        lax.fori_loop(1, at // block, body, 0)
    if last:
        low = low_lanes(rows_all)
        for j in range(GROUP // 2):
            a, b = acc_ref[2 * j], acc_ref[2 * j + 1]
            num = jnp.where(low, pltpu.roll(a, HEAD_DIM, 1), b)
            den = jnp.where(low, a, pltpu.roll(b, HEAD_DIM, 1))
            out_ref[:, j * LANES : (j + 1) * LANES] = (num / den).astype(BF16)


def post_kernel(
    core_ref, mine_ref, other_ref, pooled_ref, member_ref, w_out_ref, gain_ref, w_inner_ref, w_outer_ref, out_ref, inner_ref
):
    half = mine_ref.shape[1]
    core = core_ref[0]
    own = pl.ds(pl.multiple_of(core * half, half), half)
    far = pl.ds(pl.multiple_of((1 - core) * half, half), half)
    hidden = (
        pooled_ref[...] + mm(mine_ref[...], w_out_ref[own, :]) + mm(other_ref[...], w_out_ref[far, :])
    )
    mlp_in = (rms(hidden) * gain_ref[...]).astype(BF16)
    inner_width = w_inner_ref.shape[1]
    block = math.gcd(inner_width, 512)
    for j in range(inner_width // block):
        cols = slice(j * block, (j + 1) * block)
        inner_ref[:, cols] = gelu(mm(mlp_in, w_inner_ref[:, cols])).astype(BF16)
    region_out = (hidden + mm(inner_ref[...], w_outer_ref[...])).astype(BF16)
    slots = member_ref.shape[1]
    block = math.gcd(slots, 512)
    for i in range(slots // block):
        rows = slice(i * block, (i + 1) * block)
        out_ref[rows, :] = lax.dot_general(
            member_ref[:, rows], region_out, TN, preferred_element_type=F32
        ).astype(BF16)


def decode_kernel(tile, order, back_ref, sensors_ref, live_ref, gain_ref, w_in_ref, w_out_ref, out_ref):
    step = min(len(order), 32)
    for begin in range(0, len(order), step):
        tiles = [slice(t * tile, (t + 1) * tile) for t in order[begin : begin + step]]
        sensors = jnp.concatenate([sensors_ref[rows, :] for rows in tiles], axis=0)
        back = back_ref[begin * tile : (begin + step) * tile, :]
        total = back.astype(F32) + sensors.astype(F32)
        dec_in = (rms(total) * gain_ref[...]).astype(BF16)
        hidden = gelu(mm(dec_in, w_in_ref[...])).astype(BF16)
        result = mm(hidden, w_out_ref[...])
        for i, rows in enumerate(tiles):
            here = result[i * tile : (i + 1) * tile, :]
            out_ref[rows, :] = jnp.where(live_ref[rows, :] > 0.0, here, 0.0).astype(BF16)


def local(
    order,
    sensors,
    slot_region,
    w_query,
    w_key,
    w_value,
    w_out,
    temper,
    gain_attn,
    w_inner,
    w_outer,
    gain_mlp,
    gain_dec,
    w_dec_in,
    w_dec_out,
):
    devices = len(order)
    sen_dev, width = sensors.shape
    tile = sen_dev // devices
    me = lax.axis_index(AXIS).astype(jnp.int32).reshape(1)
    core = lax.rem(me, 2)
    bits = devices.bit_length() - 1
    pay_rows = tile * (width // LANES) + 8

    def flipped(value, mask):
        return lax.ppermute(value, AXIS, [(i, i ^ mask) for i in range(devices)])

    def exchanged(value):
        return lax.all_to_all(
            value, AXIS, split_axis=0, concat_axis=0, tiled=True, axis_index_groups=[order]
        )

    payload = pl.pallas_call(
        functools.partial(pack_kernel, tile, order),
        out_shape=jax.ShapeDtypeStruct((devices, pay_rows, LANES), BF16),
        in_specs=[SMEM, SMEM, VMEM, VMEM],
        out_specs=VMEM,
        compiler_params=PARAMS,
        name="pack",
    )(me, core, sensors, slot_region.reshape(-1, LANES))
    got = exchanged(payload)

    scale = jnp.repeat(temper * (math.log2(math.e) / HEAD_DIM), HEAD_DIM).reshape(1, -1)
    live = (slot_region >= 0).astype(F32).reshape(sen_dev, 1)

    kv_shape = jax.ShapeDtypeStruct((REG_DEV, LANES), BF16)
    pooled, members, attn_in, kv_keep, kv_send = pl.pallas_call(
        functools.partial(pool_kernel, tile),
        out_shape=(
            jax.ShapeDtypeStruct((REG_DEV, width), F32),
            jax.ShapeDtypeStruct((REG_DEV, sen_dev), BF16),
            jax.ShapeDtypeStruct((REG_DEV, width), BF16),
            kv_shape,
            kv_shape,
        ),
        in_specs=[SMEM] + [VMEM] * 4,
        out_specs=(VMEM,) * 5,
        compiler_params=PARAMS,
        name="pool",
    )(core, got, w_key, w_value, gain_attn.reshape(1, width))
    kv_other = flipped(kv_send, 1)
    slab_shape = jax.ShapeDtypeStruct((REG_DEV, GROUP * LANES), BF16)
    q_keep, q_send = pl.pallas_call(
        query_kernel,
        out_shape=(slab_shape, slab_shape),
        in_specs=[SMEM] + [VMEM] * 3,
        out_specs=(VMEM, VMEM),
        compiler_params=PARAMS,
        cost_estimate=pl.CostEstimate(
            flops=2 * REG_DEV * width * width, bytes_accessed=2 * REG_DEV * width, transcendentals=0
        ),
        name="query",
    )(core, attn_in, w_query, scale)
    kv_other, q_keep, q_send = lax.optimization_barrier((kv_other, q_keep, q_send))
    slabs = (q_keep, flipped(q_send, 1))

    def attend(parts, acc, last=False, row_parts=(0, 1)):
        keys = sum(part.shape[0] for part in parts)
        rows = len(row_parts) * REG_DEV
        acc_shape = (GROUP, rows, LANES)
        work = GROUP * rows * keys
        out_shape = (rows, GROUP * HEAD_DIM) if last else acc_shape
        return pl.pallas_call(
            functools.partial(attend_kernel, len(parts), row_parts, acc is None, last),
            out_shape=jax.ShapeDtypeStruct(out_shape, BF16 if last else F32),
            in_specs=[VMEM] * (len(row_parts) + len(parts) + (acc is not None)),
            out_specs=VMEM,
            scratch_shapes=([pltpu.VMEM(acc_shape, F32)] if last else [])
            + [pltpu.VMEM((keys, LANES), BF16)] * 2
            + [pltpu.VMEM(acc_shape, BF16)],
            compiler_params=PARAMS,
            cost_estimate=pl.CostEstimate(
                flops=work, bytes_accessed=keys * 2 * LANES, transcendentals=0
            ),
            name="attend",
        )(*(slabs[r] for r in row_parts), *parts, *(() if acc is None else (acc,)))

    one, two = 1 << (bits - 2), 1 << (bits - 1)
    own = jnp.concatenate([kv_keep, kv_other], axis=0)
    for bit in range(bits - 3, 2, -1):
        own = jnp.concatenate([own, flipped(own, 1 << bit)], axis=0)
    near, far = 1 << 1, 1 << 2

    hold = lax.optimization_barrier
    a, b = flipped(own, far), flipped(own, near)
    own_one, own_two = flipped(own, one), flipped(own, two)
    acc = attend([own], None)
    acc, a, b, own_one, own_two = hold((acc, a, b, own_one, own_two))
    ab, c = jnp.concatenate([a, b], axis=0), flipped(a, near)
    ab_one, ab_two, own_corner = flipped(ab, one), flipped(ab, two), flipped(own_two, one)
    acc = attend([ab, own_one, own_two], acc)
    acc, c, ab_one, ab_two = hold((acc, c, ab_one, ab_two))
    c_one, c_two, ab_corner = flipped(c, one), flipped(c, two), flipped(ab_one, two)
    acc = attend([c, ab_one, ab_two, own_corner], acc)
    acc, c_one, c_two = hold((acc, c_one, c_two))
    c_corner = flipped(c_two, one)
    acc = attend([c_one, c_two, ab_corner], acc)

    theirs = attend([c_corner], acc, True, (1,))
    other_heads = flipped(theirs, 1)
    mine = attend([c_corner], acc, True, (0,))
    mine, other_heads = lax.optimization_barrier((mine, other_heads))

    back = pl.pallas_call(
        post_kernel,
        out_shape=jax.ShapeDtypeStruct((sen_dev, width), BF16),
        in_specs=[SMEM] + [VMEM] * 8,
        out_specs=VMEM,
        scratch_shapes=[pltpu.VMEM((REG_DEV, w_inner.shape[1]), BF16)],
        compiler_params=PARAMS,
        name="post",
    )(core, mine, other_heads, pooled, members, w_out, gain_mlp.reshape(1, width), w_inner, w_outer)
    returned = exchanged(back.reshape(devices, tile, width)).reshape(sen_dev, width)
    return pl.pallas_call(
        functools.partial(decode_kernel, tile, order),
        out_shape=jax.ShapeDtypeStruct((sen_dev, width), BF16),
        in_specs=[VMEM] * 6,
        out_specs=VMEM,
        compiler_params=PARAMS,
        name="decode",
    )(returned, sensors, live, gain_dec.reshape(1, width), w_dec_in, w_dec_out)


def solution(mesh):
    devices, line = mesh.size, mesh.shape["dp"]
    order = sorted(range(devices), key=lambda i: (i // line, i % 2, i))
    if devices == len(ORDER):
        order = list(ORDER)
    flat = jax.sharding.Mesh(mesh.devices.reshape(-1), (AXIS,))
    placed = (P(AXIS, None), P(AXIS)) + (P(),) * 12
    return jax.shard_map(
        functools.partial(local, order),
        mesh=flat,
        in_specs=placed,
        out_specs=P(AXIS, None),
        check_vma=False,
    )
```
